128 devices in a mesh: ctx: 16 (over y, z), head: 8 (over x, core).
Axes of the slice: x: 4, y: 4, z: 4, core: 2. Of those that a mesh axis runs over, the one named last changes fastest.
Arguments:
- queries: bfloat16 [8192, 5120], P('ctx', 'head'), may hold values from -6 to 6
- key_heads: bfloat16 [8192, 1024], P('ctx', 'head'), may hold values from -6 to 6
- value_heads: bfloat16 [8192, 1024], P('ctx', 'head'), may hold values from -24 to 24
- log_gates: float32 [8192, 8], P('ctx', 'head'), may hold values from -0.75 to 0, as said below
- norm_gain: float32 [5120], P('head'), may hold values from 0.25 to 1.75
- out_weight: bfloat16 [5120, 5120], P('head'), may hold values from -0.125 to 0.125
Outputs:
- layer_out: bfloat16 [5120, 8192], P('head', 'ctx')
The draws below stay inside these ranges and needn't reach their ends.
Inputs may be any that keep to these rules, and one draw needn't show every extreme that they name: `log_gates`: every entry is negative.
All inputs are finite; a program needn't handle non-finite values.
Results may differ from the reference program's by a relative error of at most 0.017.
Values may be sent and summed in bfloat16 or wider, within the bound.
No kernel may reach another device: no remote copies, remote signals or barrier semaphores. Data moves between devices by JAX's collectives and lax.ppermute only.
A program may use at most 256 MiB of HBM per device.

```python
import math
import jax
import jax.numpy as jnp
from jax import lax

HEAD_DIM = 128
WIDTH = 5120
GROUP_HEADS = 5
TOK_DEV = 512
FEATURES = 8256
KV_HEADS = 8
QUERY_HEADS = 40
SEQ_LEN = 8192
N_CTX = 16


def draw_value_heads(key, part):
    noise_key = jax.random.fold_in(jax.random.fold_in(key, 11), 0)
    column_key = jax.random.fold_in(jax.random.fold_in(key, 11), 1)
    row_key = jax.random.fold_in(jax.random.fold_in(key, 11), 3)
    base = jax.random.normal(noise_key, (SEQ_LEN, KV_HEADS * HEAD_DIM), jnp.float32)
    column_scale = jnp.exp(jax.random.uniform(column_key, (KV_HEADS * HEAD_DIM,), jnp.float32, math.log(0.3), math.log(3.0)))
    row_scale = jnp.exp(jax.random.uniform(row_key, (SEQ_LEN, 1), jnp.float32, math.log(0.3), math.log(3.0)))
    return jnp.clip(base * column_scale[None, :] * row_scale, -24.0, 24.0).astype(jnp.bfloat16)


def draw_log_gates(key, part):
    order_key, factor_key, spot_key, amount_key = jax.random.split(jax.random.fold_in(key, 23), 4)
    order = jax.random.permutation(order_key, KV_HEADS)
    slow_count = KV_HEADS // 2
    slow = order < slow_count
    factor = jnp.exp(jax.random.uniform(factor_key, (SEQ_LEN, KV_HEADS), jnp.float32, math.log(0.5), math.log(2.0)))
    rate = jnp.where(slow, 0.7 / SEQ_LEN, 1.0 / 40.0)
    gates = -rate[None, :] * factor
    third = SEQ_LEN // 3
    spots = jax.random.randint(spot_key, (3, KV_HEADS), 0, third) + (jnp.arange(3, dtype=jnp.int32) * third)[:, None]
    amounts = jax.random.uniform(amount_key, (3, KV_HEADS), jnp.float32, math.log(0.5), math.log(0.8))
    positions = jnp.arange(SEQ_LEN, dtype=jnp.int32)
    hits = (positions[:, None, None] == spots[None, :, :]).astype(jnp.float32)
    return gates + jnp.sum(hits * amounts[None, :, :], axis=1)


def raised(result, own_key, source, target, shards_of, factor):
    owner, partner = [(jnp.arange(result.shape[position]) // (result.shape[position] // shards_of)).reshape([-1 if axis == position else 1 for axis in range(result.ndim)]) for position in (source, target)]
    chosen = jax.random.permutation(own_key, shards_of)[partner]
    strong = (owner == chosen) | (owner == (partner + shards_of // 2) % shards_of)
    return jnp.where(strong, factor * result, result)


def level_of(stream_key, dims, cuts, low, top_value):
    def one(position, blocks):
        draws = jax.random.uniform(jax.random.fold_in(jax.random.fold_in(stream_key, 6), position), (blocks,), jnp.float32, low / len(cuts), top_value / len(cuts))
        return jnp.repeat(jnp.exp(draws), dims[position] // blocks).reshape((-1,) + (1,) * (len(dims) - position - 1))

    level = one(*cuts[0])
    for cut in cuts[1:]:
        level = level * one(*cut)
    return level


def centred(key, dims, deviation, reach, shards=(), kind=jnp.bfloat16):
    array = deviation * jax.random.normal(key, dims, jnp.float32)
    if shards:
        array = array * level_of(key, dims, shards, -0.22, 0.18)
    return jnp.clip(array, -reach, reach).astype(kind)


def bell_draw_with(stream_key, dims, scale, limit, cuts, heavy, kind=jnp.bfloat16):
    entries = scale * jax.random.normal(stream_key, dims, jnp.float32)
    if cuts:
        entries = entries * level_of(stream_key, dims, cuts, -0.22, 0.18)
    return jnp.clip(raised(entries, jax.random.fold_in(stream_key, 3), *heavy), -limit, limit).astype(kind)


def setup_inputs(seed: int = 0) -> dict:
    streams_of = jax.random.split(jax.random.key(seed), 7)
    queries = centred(streams_of[0], (SEQ_LEN, QUERY_HEADS * HEAD_DIM), 1.0, 6.0, ((0, 16), (1, 8)))
    key_heads = centred(streams_of[1], (SEQ_LEN, KV_HEADS * HEAD_DIM), 1.0, 6.0, ((0, 16), (1, 8)))
    value_heads = draw_value_heads(jax.random.fold_in(streams_of[6], 71), 0)
    log_gates = draw_log_gates(jax.random.fold_in(streams_of[6], 71), 0)
    norm_gain = jnp.clip(1.0 + 0.15 * jax.random.normal(streams_of[4], (QUERY_HEADS * HEAD_DIM,), jnp.float32), 0.25, 1.75)
    out_weight = bell_draw_with(streams_of[5], (QUERY_HEADS * HEAD_DIM, WIDTH), (QUERY_HEADS * HEAD_DIM) ** -0.5, 0.125, ((0, 8),), (0, 1, 8, 2.0))
    return dict(queries=queries, key_heads=key_heads, value_heads=value_heads, log_gates=log_gates, norm_gain=norm_gain, out_weight=out_weight)


root_two = math.sqrt(2.0)

def features(vectors):
    dim_count = vectors.shape[-1]
    pieces = []
    for leading in range(dim_count):
        column = vectors[..., leading:leading + 1]
        pieces.append(column * column)
        if leading + 1 < dim_count:
            pieces.append(root_two * column * vectors[..., leading + 1:])
    return jnp.concatenate(pieces, axis=-1)

def head_block(inputs):
    query_tile, key_tile, value_tile, gate_tile, gain_tile, carry_state = inputs
    cumulative = jnp.cumsum(gate_tile)
    block_total = cumulative[-1]
    weighted = (features(key_tile.astype(jnp.float32)) * jnp.exp(block_total - cumulative)[:, None]).astype(jnp.bfloat16)
    local_sum = jnp.dot(weighted.T, value_tile, preferred_element_type=jnp.float32)
    prefix_half = carry_state.astype(jnp.bfloat16)
    token_count = query_tile.shape[0]
    qfeat = features(query_tile.astype(jnp.float32)).astype(jnp.bfloat16)
    carried = jnp.dot(qfeat.reshape(token_count * GROUP_HEADS, FEATURES), prefix_half, preferred_element_type=jnp.float32)
    carried = carried.reshape(token_count, GROUP_HEADS, HEAD_DIM) * jnp.exp(cumulative)[:, None, None]
    inner = jnp.einsum('tqh,sh->qts', query_tile.astype(jnp.float32), key_tile.astype(jnp.float32))
    positions = jnp.arange(token_count, dtype=jnp.int32)
    causal = positions[:, None] >= positions[None, :]
    weight = jnp.where(causal, jnp.exp(jnp.minimum(cumulative[:, None] - cumulative[None, :], 0.0)), 0.0)
    scores = (inner * inner * weight[None]).astype(jnp.bfloat16)
    within = jnp.einsum('qts,sd->tqd', scores.astype(jnp.float32), value_tile.astype(jnp.float32))
    numerator = carried + within
    normed = numerator * lax.rsqrt(lax.optimization_barrier(jnp.mean(numerator * numerator, axis=-1, keepdims=True)) + 1e-06) * gain_tile
    fresh_state = jnp.exp(block_total) * carry_state + local_sum
    return (normed.astype(jnp.bfloat16), fresh_state)

def reference(queries, key_heads, value_heads, log_gates, norm_gain, out_weight):
    query_blocks = queries.reshape(N_CTX, TOK_DEV, KV_HEADS, GROUP_HEADS, HEAD_DIM).transpose(0, 2, 1, 3, 4)
    key_blocks = key_heads.reshape(N_CTX, TOK_DEV, KV_HEADS, HEAD_DIM).transpose(0, 2, 1, 3)
    value_blocks = value_heads.reshape(N_CTX, TOK_DEV, KV_HEADS, HEAD_DIM).transpose(0, 2, 1, 3)
    gate_blocks = log_gates.reshape(N_CTX, TOK_DEV, KV_HEADS).transpose(0, 2, 1)
    gains = norm_gain.reshape(KV_HEADS, GROUP_HEADS, HEAD_DIM)

    def advance(states, tiles):
        query_tile, key_tile, value_tile, gate_tile = tiles
        normed, fresh = lax.map(head_block, (query_tile, key_tile, value_tile, gate_tile, gains, states))
        return (fresh, normed)
    start_states = jnp.zeros((KV_HEADS, FEATURES, HEAD_DIM), jnp.float32)
    unused, normed_all = lax.scan(advance, start_states, (query_blocks, key_blocks, value_blocks, gate_blocks))
    grouped = normed_all.transpose(1, 0, 2, 3, 4).reshape(KV_HEADS, SEQ_LEN, GROUP_HEADS * HEAD_DIM)
    weight_groups = out_weight.reshape(KV_HEADS, GROUP_HEADS * HEAD_DIM, WIDTH)

    def project(running, tiles):
        group_rows, group_weight = tiles
        group_part = jnp.dot(group_weight.T, group_rows.T, preferred_element_type=jnp.float32).astype(jnp.bfloat16)
        group_part = lax.optimization_barrier(group_part)
        return (running + group_part.astype(jnp.float32), None)
    summed, unused_too = lax.scan(project, jnp.zeros((WIDTH, SEQ_LEN), jnp.float32), (grouped, weight_groups))
    return summed.astype(jnp.bfloat16)
```

```python
import jax
import jax.numpy as jnp
from jax import lax
from jax.experimental import pallas as pl
from jax.experimental.pallas import tpu as pltpu
from jax.sharding import PartitionSpec as P

HEAD_DIM = 128
GROUP_HEADS = 5
TOK = 512
PAY = TOK + 16
SIDE = 4
CHUNK = 640
BF = jnp.bfloat16
F32 = jnp.float32
VMEM = pl.BlockSpec(memory_space=pltpu.VMEM)

CTX = SIDE * SIDE
CTX_Z = {d: [(i, (i // SIDE) * SIDE + (i + d) % SIDE) for i in range(CTX)] for d in (1, -1, 2)}
CTX_Y = {d: [(i, (i + d * SIDE) % CTX) for i in range(CTX)] for d in (1, -1)}
HEAD_X = {d: [(i, (i + 2 * d) % (2 * SIDE)) for i in range(2 * SIDE)] for d in (1, -1)}
CORE = [(i, i ^ 1) for i in range(2 * SIDE)]


def kernel_call(body, outs, flops, nbytes, scratch=(), **extra):
    return pl.pallas_call(
        body,
        out_shape=outs,
        in_specs=extra.pop("in_specs"),
        out_specs=extra.pop("out_specs", jax.tree.map(lambda _: VMEM, outs)),
        scratch_shapes=list(scratch),
        compiler_params=pltpu.CompilerParams(vmem_limit_bytes=48 * 2**20),
        cost_estimate=pl.CostEstimate(flops=flops, bytes_accessed=nbytes, transcendentals=0),
        **extra,
    )


def shape(dims, kind):
    return jax.ShapeDtypeStruct(dims, kind)


def column(row):
    return jnp.broadcast_to(row, (HEAD_DIM, TOK)).T[:, :1]


def prepare_body(key_ref, value_ref, cum_ref, out_ref):
    cum = column(cum_ref[...])
    total = cum_ref[0:1, TOK - 1 : TOK]
    out_ref[:TOK, :HEAD_DIM] = key_ref[...]
    out_ref[:TOK, HEAD_DIM:] = (value_ref[...].astype(F32) * jnp.exp(total - cum)).astype(BF)
    top = total.astype(BF).astype(F32)
    mid = (total - top).astype(BF).astype(F32)
    low = total - top - mid
    rows = lax.broadcasted_iota(jnp.int32, (16, HEAD_DIM), 0)
    lanes = lax.broadcasted_iota(jnp.int32, (16, HEAD_DIM), 1)
    tile = jnp.where(lanes == 0, top, jnp.where(lanes == 1, mid, jnp.where(lanes == 2, low, 0.0)))
    tile = jnp.where(rows == 0, tile, 0.0)
    out_ref[TOK:, :HEAD_DIM] = tile.astype(BF)
    out_ref[TOK:, HEAD_DIM:] = jnp.zeros((16, HEAD_DIM), BF)


def inner(query, key):
    return lax.dot_general(query, key, (((1,), (1,)), ((), ())), preferred_element_type=F32)


def head_cols(head):
    return slice(head * HEAD_DIM, (head + 1) * HEAD_DIM)


def own_body(query_ref, key_ref, value_ref, cum_ref, out_ref):
    cum_col = column(cum_ref[...])
    half = TOK // 2
    for part in range(2):
        rows = slice(part * half, (part + 1) * half)
        seen = (part + 1) * half
        place = part * half + lax.broadcasted_iota(jnp.int32, (half, seen), 0)
        source = lax.broadcasted_iota(jnp.int32, (half, seen), 1)
        decay = jnp.exp(jnp.minimum(cum_col[rows] - cum_ref[0:1, :seen], 0.0))
        decay = jnp.where(place >= source, decay, 0.0)
        for head in range(GROUP_HEADS):
            scores = inner(query_ref[rows, head_cols(head)], key_ref[:seen, :])
            scores = (scores * scores * decay).astype(BF)
            out_ref[rows, head_cols(head)] = jnp.dot(
                scores, value_ref[:seen, :], preferred_element_type=F32
            )


def total_of(ref, slot):
    tile = ref[slot * PAY + TOK : (slot + 1) * PAY, :HEAD_DIM].astype(F32)
    return jnp.sum(jnp.sum(tile, axis=1, keepdims=True), axis=0, keepdims=True)


def slot_places(place_z):
    return [place_z, (place_z + 3) % SIDE, (place_z + 1) % SIDE, (place_z + 2) % SIDE]


def gated(condition, value):
    return jnp.where(condition, value, jnp.zeros_like(value))


def later_sums(places, totals):
    return [
        sum(gated(places[i] > places[k], totals[i]) for i in range(SIDE) if i != k)
        for k in range(SIDE)
    ]


def add_slots(query_ref, pieces, acc_ref, scaled):
    for first in range(0, len(pieces), 2):
        pair = pieces[first : first + 2]
        keys = []
        for index, (ref, slot, log_decay) in enumerate(pair):
            rows = slice(slot * PAY, slot * PAY + TOK)
            values = ref[rows, HEAD_DIM:].astype(F32) * jnp.exp(log_decay)
            scaled[index * TOK : (index + 1) * TOK, :] = values.astype(BF)
            keys.append(ref[rows, :HEAD_DIM])
        key = jnp.concatenate(keys, axis=0)
        value = scaled[: len(pair) * TOK, :]
        for head in range(GROUP_HEADS):
            scores = inner(query_ref[:, head_cols(head)], key)
            scores = (scores * scores).astype(BF)
            acc_ref[:, head_cols(head)] += jnp.dot(scores, value, preferred_element_type=F32)


def row_body(query_ref, own_ref, back_ref, ahead_ref, far_ref, acc_ref, stat_ref, scaled):
    place_z = lax.axis_index("ctx") % SIDE
    places = slot_places(place_z)
    refs = [own_ref, back_ref, ahead_ref, far_ref]
    totals = [total_of(ref, 0) for ref in refs]
    acc_ref[...] = jnp.zeros_like(acc_ref)
    before = sum(gated(places[k] < place_z, totals[k]) for k in range(1, SIDE))
    stat_ref[...] = jnp.broadcast_to(before, stat_ref.shape)
    for k in range(1, SIDE):
        log_decay = sum(
            gated((places[i] > places[k]) & (places[i] < place_z), totals[i])
            for i in range(1, SIDE)
            if i != k
        )

        @pl.when(places[k] < place_z)
        def _():
            add_slots(query_ref, [(refs[k], 0, log_decay)], acc_ref, scaled)


def near_body(query_ref, back_ref, ahead_ref, stat_ref, acc_in, acc_ref, wrap_ref, out_stat, scaled):
    index = lax.axis_index("ctx")
    place_y, places = index // SIDE, slot_places(index % SIDE)
    before = stat_ref[0:1, 0:1]
    totals = [total_of(back_ref, k) for k in range(SIDE)]
    later = later_sums(places, totals)
    out_stat[...] = jnp.broadcast_to(before + sum(totals), out_stat.shape)
    acc_ref[...] = acc_in[...]

    @pl.when(place_y >= 1)
    def _():
        add_slots(query_ref, [(back_ref, k, before + later[k]) for k in range(SIDE)], acc_ref, scaled)

    wrap_later = later_sums(places, [total_of(ahead_ref, k) for k in range(SIDE)])

    @pl.when(place_y == SIDE - 1)
    def _():
        wrap_ref[...] = jnp.zeros_like(wrap_ref)
        add_slots(query_ref, [(ahead_ref, k, wrap_later[k]) for k in range(SIDE)], wrap_ref, scaled)


def last_body(
    query_ref, low_ref, high_ref, stat_ref, acc_in, wrap_ref, own_ref, cum_ref, gain_ref, out_ref, acc, scaled
):
    index = lax.axis_index("ctx")
    place_y, places = index // SIDE, slot_places(index % SIDE)
    before = stat_ref[0:1, 0:1]
    where = [(low_ref, 0), (low_ref, 1), (high_ref, 0), (high_ref, 1)]
    totals = [total_of(*pair) for pair in where]
    later = later_sums(places, totals)
    acc[...] = acc_in[...]

    @pl.when(place_y == SIDE - 1)
    def _():
        acc[...] += jnp.exp(before + sum(totals)) * wrap_ref[...]

    @pl.when(place_y >= 2)
    def _():
        add_slots(query_ref, [(*where[k], before + later[k]) for k in range(SIDE)], acc, scaled)

    grow = jnp.exp(column(cum_ref[...]))
    for head in range(GROUP_HEADS):
        cols = head_cols(head)
        number = own_ref[:, cols] + grow * acc[:, cols]
        mean = jnp.mean(number * number, axis=-1, keepdims=True)
        out_ref[:, cols] = (number * lax.rsqrt(mean + 1e-06) * gain_ref[0:1, cols]).astype(BF)


def project(normed, weight, flip):
    place = lax.axis_index("head").reshape(1)

    def chunk_of(step, place):
        turn = jnp.where(step == 3, 0, jnp.where(step == 2, 3, 2 - step))
        return ((place[0] >> 1) + turn & 3) * 2 + ((place[0] & 1) ^ flip)

    def body(place_ref, normed_ref, weight_ref, out_ref):
        out_ref[0] = jnp.dot(
            normed_ref[...], weight_ref[...], preferred_element_type=F32
        ).astype(BF)

    return pl.pallas_call(
        body,
        out_shape=shape((SIDE, TOK, CHUNK), BF),
        grid_spec=pltpu.PrefetchScalarGridSpec(
            num_scalar_prefetch=1,
            grid=(SIDE,),
            in_specs=[
                pl.BlockSpec((TOK, CHUNK), lambda i, c: (0, 0)),
                pl.BlockSpec((CHUNK, CHUNK), lambda i, c: (0, chunk_of(i, c))),
            ],
            out_specs=pl.BlockSpec((1, TOK, CHUNK), lambda i, c: (i, 0, 0)),
        ),
        compiler_params=pltpu.CompilerParams(vmem_limit_bytes=48 * 2**20),
        cost_estimate=pl.CostEstimate(
            flops=2 * TOK * CHUNK * CHUNK * SIDE, bytes_accessed=6 * 2**20, transcendentals=0
        ),
    )(place, normed, weight)


def presum_body(mine_ref, other_ref, far_r, far_l, near_r, near_l, hold_r, hold_l, own_ref):
    half = TOK // 2

    def both(chunk, rows):
        return mine_ref[chunk, rows, :].astype(F32) + other_ref[chunk, rows, :].astype(F32)

    low, high = slice(0, half), slice(half, TOK)
    far_r[...] = both(0, low).astype(BF)
    far_l[...] = both(0, high).astype(BF)
    near_r[...] = both(1, high).astype(BF)
    near_l[...] = both(2, low).astype(BF)
    hold_r[...] = both(1, low)
    hold_l[...] = both(2, high)
    own_ref[...] = both(3, slice(0, TOK))


def pass_body(hold_r, far_r, hold_l, far_l, out_r, out_l):
    out_r[...] = (hold_r[...] + far_r[...].astype(F32)).astype(BF)
    out_l[...] = (hold_l[...] + far_l[...].astype(F32)).astype(BF)


def finish_body(own_ref, sum_r, sum_l, near_r, near_l, out_ref):
    half = TOK // 2
    low = own_ref[:half, :] + sum_r[...].astype(F32) + near_l[...].astype(F32)
    high = own_ref[half:, :] + sum_l[...].astype(F32) + near_r[...].astype(F32)
    out_ref[:, :half] = low.T.astype(BF)
    out_ref[:, half:] = high.T.astype(BF)


def per_device(queries, key_heads, value_heads, log_gates, norm_gain, out_weight):
    wide = GROUP_HEADS * HEAD_DIM
    cum = jnp.cumsum(log_gates[:, 0]).reshape(1, TOK)
    payload = kernel_call(
        prepare_body, shape((PAY, 2 * HEAD_DIM), BF), 2**18, 2**19, in_specs=[VMEM] * 3
    )(key_heads, value_heads, cum)
    back, ahead, far = (lax.ppermute(payload, "ctx", CTX_Z[d]) for d in (1, -1, 2))
    block_flops = 4 * TOK * TOK * wide
    own = kernel_call(own_body, shape((TOK, wide), F32), block_flops, 2**21, in_specs=[VMEM] * 4)(
        queries, key_heads, value_heads, cum
    )
    row = jnp.concatenate([payload, back, ahead, far], axis=0)
    row_back, row_ahead = (lax.ppermute(row, "ctx", CTX_Y[d]) for d in (1, -1))
    acc_shape = shape((TOK, wide), F32)
    stat_shape = shape((8, HEAD_DIM), F32)
    scaled = pltpu.VMEM((2 * TOK, HEAD_DIM), BF)
    acc, stat = kernel_call(
        row_body, (acc_shape, stat_shape), 3 * block_flops, 2**21, [scaled], in_specs=[VMEM] * 5
    )(queries, payload, back, ahead, far)
    two = 2 * PAY
    low = lax.ppermute(row_back[:two], "ctx", CTX_Y[1])
    high = lax.ppermute(row_ahead[two:], "ctx", CTX_Y[-1])
    acc, wrap, stat = kernel_call(
        near_body,
        (acc_shape, acc_shape, stat_shape),
        8 * block_flops,
        2**22,
        [scaled],
        in_specs=[VMEM] * 5,
    )(queries, row_back, row_ahead, stat, acc)
    normed = kernel_call(
        last_body,
        shape((TOK, wide), BF),
        4 * block_flops,
        2**22,
        [pltpu.VMEM((TOK, wide), F32), scaled],
        in_specs=[VMEM] * 9,
    )(queries, low, high, stat, acc, wrap, own, cum, norm_gain.reshape(1, wide))

    other = lax.ppermute(project(normed, out_weight, 1), "head", CORE)
    mine = project(normed, out_weight, 0)
    half_bf, half_f32 = shape((TOK // 2, CHUNK), BF), shape((TOK // 2, CHUNK), F32)
    far_r, far_l, near_r, near_l, hold_r, hold_l, own_sum = kernel_call(
        presum_body,
        (half_bf,) * 4 + (half_f32,) * 2 + (shape((TOK, CHUNK), F32),),
        2**21,
        2**23,
        in_specs=[VMEM] * 2,
    )(mine, other)
    far_r = lax.ppermute(far_r, "head", HEAD_X[1])
    far_l = lax.ppermute(far_l, "head", HEAD_X[-1])
    near_r = lax.ppermute(near_r, "head", HEAD_X[1])
    near_l = lax.ppermute(near_l, "head", HEAD_X[-1])
    sum_r, sum_l = kernel_call(pass_body, (half_bf,) * 2, 2**19, 2**21, in_specs=[VMEM] * 4)(
        hold_r, far_r, hold_l, far_l
    )
    sum_r = lax.ppermute(sum_r, "head", HEAD_X[1])
    sum_l = lax.ppermute(sum_l, "head", HEAD_X[-1])
    return kernel_call(finish_body, shape((CHUNK, TOK), BF), 2**20, 2**22, in_specs=[VMEM] * 5)(
        own_sum, sum_r, sum_l, near_r, near_l
    )


def solution(mesh):
    return jax.shard_map(
        per_device,
        mesh=mesh,
        in_specs=(
            P("ctx", "head"),
            P("ctx", "head"),
            P("ctx", "head"),
            P("ctx", "head"),
            P("head"),
            P("head", None),
        ),
        out_specs=P("head", "ctx"),
        check_vma=False,
    )
```

```python
import jax
import jax.numpy as jnp
from jax import lax
from jax.experimental import pallas as pl
from jax.experimental.pallas import tpu as pltpu
from jax.sharding import PartitionSpec as P

HEAD_DIM = 128
GROUP_HEADS = 5
TOK = 512
PAY = TOK + 16
SIDE = 4
CHUNK = 640
BF = jnp.bfloat16
F32 = jnp.float32
VMEM = pl.BlockSpec(memory_space=pltpu.VMEM)

CTX = SIDE * SIDE
CTX_Z = {d: [(i, (i // SIDE) * SIDE + (i + d) % SIDE) for i in range(CTX)] for d in (1, -1)}
CTX_Y = {d: [(i, (i + d * SIDE) % CTX) for i in range(CTX)] for d in (1, -1)}
HEAD_X = {d: [(i, (i + 2 * d) % (2 * SIDE)) for i in range(2 * SIDE)] for d in (1, -1)}
CORE = [(i, i ^ 1) for i in range(2 * SIDE)]


def kernel_call(body, outs, flops, nbytes, scratch=(), **extra):
    return pl.pallas_call(
        body,
        out_shape=outs,
        in_specs=extra.pop("in_specs"),
        out_specs=extra.pop("out_specs", jax.tree.map(lambda _: VMEM, outs)),
        scratch_shapes=list(scratch),
        compiler_params=pltpu.CompilerParams(vmem_limit_bytes=24 * 2**20),
        cost_estimate=pl.CostEstimate(flops=flops, bytes_accessed=nbytes, transcendentals=0),
        **extra,
    )


def shape(dims, kind):
    return jax.ShapeDtypeStruct(dims, kind)


def column(row):
    return jnp.broadcast_to(row, (HEAD_DIM, TOK)).T[:, :1]


def prepare_body(key_ref, value_ref, gate_ref, out_ref, cum_ref):
    gates = gate_ref[...]
    top = gates.astype(BF).astype(F32)
    mid = (gates - top).astype(BF).astype(F32)
    rows = lax.broadcasted_iota(jnp.int32, (16, TOK), 0)
    parts = jnp.where(rows == 0, top, jnp.where(rows == 1, mid, gates - top - mid))
    parts = jnp.where(rows < 3, parts, 0.0).astype(BF)
    source = lax.broadcasted_iota(jnp.int32, (TOK, TOK), 0)
    place = lax.broadcasted_iota(jnp.int32, (TOK, TOK), 1)
    upto = jnp.where(source <= place, 1.0, 0.0).astype(BF)
    sums = jnp.dot(parts, upto, preferred_element_type=F32)
    cum = jnp.sum(sums, axis=0, keepdims=True)
    cum_ref[...] = cum
    total = cum[:, TOK - 1 :]
    out_ref[:TOK, :HEAD_DIM] = key_ref[...]
    out_ref[:TOK, HEAD_DIM:] = (value_ref[...].astype(F32) * jnp.exp(total - column(cum))).astype(BF)
    top = total.astype(BF).astype(F32)
    mid = (total - top).astype(BF).astype(F32)
    rows = lax.broadcasted_iota(jnp.int32, (16, HEAD_DIM), 0)
    lanes = lax.broadcasted_iota(jnp.int32, (16, HEAD_DIM), 1)
    tile = jnp.where(lanes == 0, top, jnp.where(lanes == 1, mid, jnp.where(lanes == 2, total - top - mid, 0.0)))
    out_ref[TOK:, :HEAD_DIM] = jnp.where(rows == 0, tile, 0.0).astype(BF)
    out_ref[TOK:, HEAD_DIM:] = jnp.zeros((16, HEAD_DIM), BF)


def inner(query, key):
    return lax.dot_general(query, key, (((1,), (1,)), ((), ())), preferred_element_type=F32)


def head_cols(head):
    return slice(head * HEAD_DIM, (head + 1) * HEAD_DIM)


def own_body(query_ref, key_ref, value_ref, cum_ref, out_ref):
    cum_col = column(cum_ref[...])
    half = TOK // 2
    for part in range(2):
        rows = slice(part * half, (part + 1) * half)
        seen = (part + 1) * half
        place = part * half + lax.broadcasted_iota(jnp.int32, (half, seen), 0)
        source = lax.broadcasted_iota(jnp.int32, (half, seen), 1)
        decay = jnp.exp(jnp.minimum(cum_col[rows] - cum_ref[0:1, :seen], 0.0))
        decay = jnp.where(place >= source, decay, 0.0)
        for head in range(GROUP_HEADS):
            scores = inner(query_ref[rows, head_cols(head)], key_ref[:seen, :])
            scores = (scores * scores * decay).astype(BF)
            out_ref[rows, head_cols(head)] = jnp.dot(
                scores, value_ref[:seen, :], preferred_element_type=F32
            )


def total_of(ref, slot):
    tile = ref[slot * PAY + TOK : (slot + 1) * PAY, :HEAD_DIM].astype(F32)
    return jnp.sum(jnp.sum(tile, axis=1, keepdims=True), axis=0, keepdims=True)


def slot_places(place_z):
    return [place_z, (place_z + 3) % SIDE, (place_z + 1) % SIDE, (place_z + 2) % SIDE]


def gated(condition, value):
    return jnp.where(condition, value, jnp.zeros_like(value))


def later_sums(places, totals):
    return [
        sum(gated(places[i] > places[k], totals[i]) for i in range(SIDE) if i != k)
        for k in range(SIDE)
    ]


def add_slots(query_ref, pieces, acc_ref, scaled):
    for first in range(0, len(pieces), 2):
        pair = pieces[first : first + 2]
        keys = []
        for index, (ref, slot, log_decay) in enumerate(pair):
            rows = slice(slot * PAY, slot * PAY + TOK)
            values = ref[rows, HEAD_DIM:].astype(F32) * jnp.exp(log_decay)
            scaled[index * TOK : (index + 1) * TOK, :] = values.astype(BF)
            keys.append(ref[rows, :HEAD_DIM])
        key = jnp.concatenate(keys, axis=0)
        value = scaled[: len(pair) * TOK, :]
        for head in range(GROUP_HEADS):
            scores = inner(query_ref[:, head_cols(head)], key)
            scores = (scores * scores).astype(BF)
            acc_ref[:, head_cols(head)] += jnp.dot(scores, value, preferred_element_type=F32)


def row_body(query_ref, own_ref, back_ref, ahead_ref, far_ref, acc_ref, stat_ref, scaled):
    place_z = lax.axis_index("ctx") % SIDE
    places = slot_places(place_z)
    refs = [own_ref, back_ref, ahead_ref, far_ref]
    totals = [total_of(ref, 0) for ref in refs]
    acc_ref[...] = jnp.zeros_like(acc_ref)
    before = sum(gated(places[k] < place_z, totals[k]) for k in range(1, SIDE))
    stat_ref[...] = jnp.broadcast_to(before, stat_ref.shape)
    for k in range(1, SIDE):
        log_decay = sum(
            gated((places[i] > places[k]) & (places[i] < place_z), totals[i])
            for i in range(1, SIDE)
            if i != k
        )

        @pl.when(places[k] < place_z)
        def _():
            add_slots(query_ref, [(refs[k], 0, log_decay)], acc_ref, scaled)


def first_body(query_ref, back_ref, ahead_ref, back_acc, ahead_acc, scaled):
    place_y = lax.axis_index("ctx") // SIDE
    back_acc[...] = jnp.zeros_like(back_acc)
    ahead_acc[...] = jnp.zeros_like(ahead_acc)
    zero = jnp.zeros((1, 1), F32)

    @pl.when(place_y >= 1)
    def _():
        add_slots(query_ref, [(back_ref, 0, zero)], back_acc, scaled)

    @pl.when(place_y == SIDE - 1)
    def _():
        add_slots(query_ref, [(ahead_ref, 0, zero)], ahead_acc, scaled)


def row_slots(first, middle, far):
    return [(first, 0), (middle, 0), (middle, 1), (far, 0)]


def near_body(
    query_ref, back0, back12, back3, ahead0, ahead12, ahead3, stat_ref, acc_in, back_in, wrap_in,
    acc_ref, wrap_ref, out_stat, scaled
):
    index = lax.axis_index("ctx")
    place_y, places = index // SIDE, slot_places(index % SIDE)
    before = stat_ref[0:1, 0:1]
    slots = row_slots(back0, back12, back3)
    totals = [total_of(*slot) for slot in slots]
    later = later_sums(places, totals)
    out_stat[...] = jnp.broadcast_to(before + sum(totals), out_stat.shape)
    acc_ref[...] = acc_in[...] + jnp.exp(before + later[0]) * back_in[...]

    @pl.when(place_y >= 1)
    def _():
        add_slots(
            query_ref, [(*slots[k], before + later[k]) for k in range(1, SIDE)], acc_ref, scaled
        )

    @pl.when(place_y == SIDE - 1)
    def _():
        slots = row_slots(ahead0, ahead12, ahead3)
        later = later_sums(places, [total_of(*slot) for slot in slots])
        wrap_ref[...] = jnp.exp(later[0]) * wrap_in[...]
        add_slots(query_ref, [(*slots[k], later[k]) for k in range(1, SIDE)], wrap_ref, scaled)


def last_body(
    query_ref, far0, far12, far3, stat_ref, acc_in, wrap_ref, own_ref, cum_ref, gain_ref,
    out_ref, acc, scaled
):
    index = lax.axis_index("ctx")
    place_y, places = index // SIDE, slot_places(index % SIDE)
    before = stat_ref[0:1, 0:1]
    slots = row_slots(far0, far12, far3)
    totals = [total_of(*slot) for slot in slots]
    later = later_sums(places, totals)
    acc[...] = acc_in[...]

    @pl.when(place_y == SIDE - 1)
    def _():
        acc[...] += jnp.exp(before + sum(totals)) * wrap_ref[...]

    @pl.when(place_y >= 2)
    def _():
        add_slots(query_ref, [(*slots[k], before + later[k]) for k in range(SIDE)], acc, scaled)

    grow = jnp.exp(column(cum_ref[...]))
    for head in range(GROUP_HEADS):
        cols = head_cols(head)
        number = own_ref[:, cols] + grow * acc[:, cols]
        mean = jnp.mean(number * number, axis=-1, keepdims=True)
        out_ref[:, cols] = (number * lax.rsqrt(mean + 1e-06) * gain_ref[0:1, cols]).astype(BF)


def features_of(weight_ref, step, flip):
    place = lax.axis_index("head")
    chunk = (place // 2 + step) % SIDE * 2 + (place % 2 + flip) % 2
    return weight_ref[:, pl.ds(pl.multiple_of(chunk * CHUNK, HEAD_DIM), CHUNK)]


def product(normed_ref, weight_ref, step, flip):
    return jnp.dot(
        normed_ref[...], features_of(weight_ref, step, flip), preferred_element_type=F32
    )


def other_far_body(normed_ref, weight_ref, out_ref):
    out_ref[...] = product(normed_ref, weight_ref, 2, 1).astype(BF)


def other_near_body(normed_ref, weight_ref, out_ref):
    for slot, step in enumerate((1, 3, 0)):
        out_ref[slot] = product(normed_ref, weight_ref, step, 1).astype(BF)


def mine_far_body(normed_ref, weight_ref, other_ref, far_r, far_l):
    half = TOK // 2
    both = product(normed_ref, weight_ref, 2, 0) + other_ref[...].astype(F32)
    far_r[...] = both[:half].astype(BF)
    far_l[...] = both[half:].astype(BF)


def mine_near_body(normed_ref, weight_ref, other_ref, near_r, near_l, hold_r, hold_l, own_ref):
    half = TOK // 2
    both = product(normed_ref, weight_ref, 1, 0) + other_ref[0].astype(F32)
    hold_r[...] = both[:half]
    near_r[...] = both[half:].astype(BF)
    both = product(normed_ref, weight_ref, 3, 0) + other_ref[1].astype(F32)
    near_l[...] = both[:half].astype(BF)
    hold_l[...] = both[half:]
    own_ref[...] = product(normed_ref, weight_ref, 0, 0) + other_ref[2].astype(F32)


def pass_body(hold_r, far_r, hold_l, far_l, out_r, out_l):
    out_r[...] = (hold_r[...] + far_r[...].astype(F32)).astype(BF)
    out_l[...] = (hold_l[...] + far_l[...].astype(F32)).astype(BF)


def gather_body(own_ref, near_r, near_l, out_ref):
    half = TOK // 2
    out_ref[:half, :] = own_ref[:half, :] + near_l[...].astype(F32)
    out_ref[half:, :] = own_ref[half:, :] + near_r[...].astype(F32)


def finish_body(own_ref, sum_r, sum_l, out_ref):
    half = TOK // 2
    out_ref[:, :half] = (own_ref[:half, :] + sum_r[...].astype(F32)).T.astype(BF)
    out_ref[:, half:] = (own_ref[half:, :] + sum_l[...].astype(F32)).T.astype(BF)


def send(value, axis, pairs):
    return lax.ppermute(value, axis, pairs)


def per_device(queries, key_heads, value_heads, log_gates, norm_gain, out_weight):
    wide = GROUP_HEADS * HEAD_DIM
    after = lax.optimization_barrier
    payload, cum = kernel_call(
        prepare_body,
        (shape((PAY, 2 * HEAD_DIM), BF), shape((1, TOK), F32)),
        2**23,
        2**19,
        in_specs=[VMEM] * 3,
    )(key_heads, value_heads, log_gates.reshape(1, TOK))
    row_back = send(payload, "ctx", CTX_Z[1])
    row_ahead = send(payload, "ctx", CTX_Z[-1])
    back0 = send(payload, "ctx", CTX_Y[1])
    ahead0 = send(payload, "ctx", CTX_Y[-1])
    block_flops = 4 * TOK * TOK * wide
    acc_shape, stat_shape = shape((TOK, wide), F32), shape((8, HEAD_DIM), F32)
    scaled = pltpu.VMEM((2 * TOK, HEAD_DIM), BF)
    own = kernel_call(own_body, acc_shape, block_flops, 2**21, in_specs=[VMEM] * 4)(
        queries, key_heads, value_heads, cum
    )
    row_far = send(row_back, "ctx", CTX_Z[1])
    middle = jnp.concatenate([row_back, row_ahead], axis=0)
    middle, own = after((middle, own))
    back12 = send(middle, "ctx", CTX_Y[1])
    ahead12 = send(middle, "ctx", CTX_Y[-1])
    back_acc, wrap = kernel_call(
        first_body, (acc_shape, acc_shape), 2 * block_flops, 2**21, [scaled], in_specs=[VMEM] * 3
    )(queries, back0, ahead0)
    far_out, back_acc, wrap = after((row_far, back_acc, wrap))
    back3 = send(far_out, "ctx", CTX_Y[1])
    ahead3 = send(far_out, "ctx", CTX_Y[-1])
    acc, stat = kernel_call(
        row_body, (acc_shape, stat_shape), 3 * block_flops, 2**21, [scaled], in_specs=[VMEM] * 5
    )(queries, payload, row_back, row_ahead, row_far)
    pass12, acc = after((back12, acc))
    far12 = send(pass12, "ctx", CTX_Y[1])
    far0 = send(ahead0, "ctx", CTX_Y[-1])
    far3 = send(ahead3, "ctx", CTX_Y[-1])
    acc, wrap, stat = kernel_call(
        near_body,
        (acc_shape, acc_shape, stat_shape),
        6 * block_flops,
        2**22,
        [scaled],
        in_specs=[VMEM] * 11,
    )(queries, back0, back12, back3, ahead0, ahead12, ahead3, stat, acc, back_acc, wrap)
    normed = kernel_call(
        last_body,
        shape((TOK, wide), BF),
        4 * block_flops,
        2**22,
        [pltpu.VMEM((TOK, wide), F32), scaled],
        in_specs=[VMEM] * 10,
    )(queries, far0, far12, far3, stat, acc, wrap, own, cum, norm_gain.reshape(1, wide))

    chunk_flops = 2 * TOK * CHUNK * wide
    chunk = shape((TOK, CHUNK), BF)
    half_bf, half_f32 = shape((TOK // 2, CHUNK), BF), shape((TOK // 2, CHUNK), F32)
    other_far = kernel_call(other_far_body, chunk, chunk_flops, 2**20, in_specs=[VMEM] * 2)(
        normed, out_weight
    )
    normed, other_far = after((normed, other_far))
    other_far = send(other_far, "head", CORE)
    other_near = kernel_call(
        other_near_body, shape((3, TOK, CHUNK), BF), 30 * chunk_flops, 2**21, in_specs=[VMEM] * 2
    )(normed, out_weight)
    other_near = send(other_near, "head", CORE)
    far_r, far_l = kernel_call(
        mine_far_body, (half_bf, half_bf), 30 * chunk_flops, 2**20, in_specs=[VMEM] * 3
    )(normed, out_weight, other_far)
    far_r = send(far_r, "head", HEAD_X[1])
    far_l = send(far_l, "head", HEAD_X[-1])
    near_r, near_l, hold_r, hold_l, own_sum = kernel_call(
        mine_near_body,
        (half_bf, half_bf, half_f32, half_f32, shape((TOK, CHUNK), F32)),
        3 * chunk_flops,
        2**22,
        in_specs=[VMEM] * 3,
    )(normed, out_weight, other_near)
    near_r = send(near_r, "head", HEAD_X[1])
    near_l = send(near_l, "head", HEAD_X[-1])
    sum_r, sum_l = kernel_call(pass_body, (half_bf,) * 2, 2**19, 2**21, in_specs=[VMEM] * 4)(
        hold_r, far_r, hold_l, far_l
    )
    sum_r = send(sum_r, "head", HEAD_X[1])
    sum_l = send(sum_l, "head", HEAD_X[-1])
    own_sum = kernel_call(
        gather_body, shape((TOK, CHUNK), F32), 2**20, 2**22, in_specs=[VMEM] * 3
    )(own_sum, near_r, near_l)
    return kernel_call(finish_body, shape((CHUNK, TOK), BF), 2**20, 2**22, in_specs=[VMEM] * 3)(
        own_sum, sum_r, sum_l
    )


def solution(mesh):
    return jax.shard_map(
        per_device,
        mesh=mesh,
        in_specs=(
            P("ctx", "head"),
            P("ctx", "head"),
            P("ctx", "head"),
            P("ctx", "head"),
            P("head"),
            P("head", None),
        ),
        out_specs=P("head", "ctx"),
        check_vma=False,
    )
```

```python
import jax
import jax.numpy as jnp
from jax import lax
from jax.experimental import pallas as pl
from jax.experimental.pallas import tpu as pltpu
from jax.sharding import PartitionSpec as P

HEAD_DIM = 128
GROUP_HEADS = 5
TOK = 512
PAY = TOK + 16
SIDE = 4
CHUNK = 640
BF = jnp.bfloat16
F32 = jnp.float32
VMEM = pl.BlockSpec(memory_space=pltpu.VMEM)

CTX = SIDE * SIDE
CTX_Z = {d: [(i, (i // SIDE) * SIDE + (i + d) % SIDE) for i in range(CTX)] for d in (1, -1)}
CTX_Y = {d: [(i, (i + d * SIDE) % CTX) for i in range(CTX)] for d in (1, -1, 2)}
HEAD_X = {d: [(i, (i + 2 * d) % (2 * SIDE)) for i in range(2 * SIDE)] for d in (1, -1)}
CORE = [(i, i ^ 1) for i in range(2 * SIDE)]


def kernel_call(body, outs, flops, nbytes, scratch=(), **extra):
    return pl.pallas_call(
        body,
        out_shape=outs,
        in_specs=extra.pop("in_specs"),
        out_specs=extra.pop("out_specs", jax.tree.map(lambda _: VMEM, outs)),
        scratch_shapes=list(scratch),
        compiler_params=pltpu.CompilerParams(vmem_limit_bytes=24 * 2**20),
        cost_estimate=pl.CostEstimate(flops=flops, bytes_accessed=nbytes, transcendentals=0),
        **extra,
    )


def shape(dims, kind):
    return jax.ShapeDtypeStruct(dims, kind)


def column(row):
    return jnp.broadcast_to(row, (HEAD_DIM, TOK)).T[:, :1]


def prepare_body(key_hbm, value_hbm, gate_hbm, out_ref, cum_ref, value_ref, gate_ref, sems):
    copies = [
        pltpu.make_async_copy(gate_hbm, gate_ref, sems.at[0]),
        pltpu.make_async_copy(value_hbm, value_ref, sems.at[1]),
        pltpu.make_async_copy(key_hbm, out_ref.at[pl.ds(0, TOK), pl.ds(0, HEAD_DIM)], sems.at[2]),
    ]
    for copy in copies:
        copy.start()
    copies[0].wait()
    gates = gate_ref[...]
    top = gates.astype(BF).astype(F32)
    mid = (gates - top).astype(BF).astype(F32)
    rows = lax.broadcasted_iota(jnp.int32, (16, TOK), 0)
    parts = jnp.where(rows == 0, top, jnp.where(rows == 1, mid, gates - top - mid))
    parts = jnp.where(rows < 3, parts, 0.0).astype(BF)
    source = lax.broadcasted_iota(jnp.int32, (TOK, TOK), 0)
    place = lax.broadcasted_iota(jnp.int32, (TOK, TOK), 1)
    upto = jnp.where(source <= place, 1.0, 0.0).astype(BF)
    sums = jnp.dot(parts, upto, preferred_element_type=F32)
    cum = jnp.sum(sums, axis=0, keepdims=True)
    cum_ref[...] = cum
    total = cum[:, TOK - 1 :]
    copies[1].wait()
    out_ref[:TOK, HEAD_DIM:] = (value_ref[...].astype(F32) * jnp.exp(total - column(cum))).astype(BF)
    top = total.astype(BF).astype(F32)
    mid = (total - top).astype(BF).astype(F32)
    rows = lax.broadcasted_iota(jnp.int32, (16, HEAD_DIM), 0)
    lanes = lax.broadcasted_iota(jnp.int32, (16, HEAD_DIM), 1)
    tile = jnp.where(lanes == 0, top, jnp.where(lanes == 1, mid, jnp.where(lanes == 2, total - top - mid, 0.0)))
    out_ref[TOK:, :HEAD_DIM] = jnp.where(rows == 0, tile, 0.0).astype(BF)
    out_ref[TOK:, HEAD_DIM:] = jnp.zeros((16, HEAD_DIM), BF)
    copies[2].wait()


def inner(query, key):
    return lax.dot_general(query, key, (((1,), (1,)), ((), ())), preferred_element_type=F32)


def head_cols(head):
    return slice(head * HEAD_DIM, (head + 1) * HEAD_DIM)


def own_body(query_ref, key_ref, value_ref, cum_ref, out_ref):
    cum_col = column(cum_ref[...])
    half = TOK // 2
    for part in range(2):
        rows = slice(part * half, (part + 1) * half)
        seen = (part + 1) * half
        place = part * half + lax.broadcasted_iota(jnp.int32, (half, seen), 0)
        source = lax.broadcasted_iota(jnp.int32, (half, seen), 1)
        decay = jnp.exp(jnp.minimum(cum_col[rows] - cum_ref[0:1, :seen], 0.0))
        decay = jnp.where(place >= source, decay, 0.0)
        for head in range(GROUP_HEADS):
            scores = inner(query_ref[rows, head_cols(head)], key_ref[:seen, :])
            scores = (scores * scores * decay).astype(BF)
            out_ref[rows, head_cols(head)] = jnp.dot(
                scores, value_ref[:seen, :], preferred_element_type=F32
            )


def total_of(ref, slot):
    tile = ref[slot * PAY + TOK : (slot + 1) * PAY, :HEAD_DIM].astype(F32)
    return jnp.sum(jnp.sum(tile, axis=1, keepdims=True), axis=0, keepdims=True)


def slot_places(place_z):
    return [place_z, (place_z + 3) % SIDE, (place_z + 1) % SIDE, (place_z + 2) % SIDE]


def gated(condition, value):
    return jnp.where(condition, value, jnp.zeros_like(value))


def later_sums(places, totals):
    return [
        sum(gated(places[i] > places[k], totals[i]) for i in range(SIDE) if i != k)
        for k in range(SIDE)
    ]


def stage(slot, log_decay, place, keys, values):
    ref, index = slot
    rows = slice(index * PAY, index * PAY + TOK)
    target = slice(place * TOK, (place + 1) * TOK)
    keys[target, :] = ref[rows, :HEAD_DIM]
    values[target, :] = (ref[rows, HEAD_DIM:].astype(F32) * jnp.exp(log_decay)).astype(BF)


def attend(query_ref, keys, values, start, size, acc_ref):
    rows = pl.ds(pl.multiple_of(start, size), size)
    key, value = keys[rows, :], values[rows, :]
    for head in range(GROUP_HEADS):
        scores = inner(query_ref[:, head_cols(head)], key)
        scores = (scores * scores).astype(BF)
        acc_ref[:, head_cols(head)] += jnp.dot(scores, value, preferred_element_type=F32)


def row_body(query_ref, own_ref, back_ref, ahead_ref, far_ref, acc_ref, stat_ref, keys, values):
    place_z = lax.axis_index("ctx") % SIDE
    places = slot_places(place_z)
    refs = [own_ref, back_ref, ahead_ref, far_ref]
    totals = [total_of(ref, 0) for ref in refs]
    acc_ref[...] = jnp.zeros_like(acc_ref)
    before = sum(gated(places[k] < place_z, totals[k]) for k in range(1, SIDE))
    stat_ref[...] = jnp.broadcast_to(before, stat_ref.shape)
    for k in range(1, SIDE):
        log_decay = sum(
            gated((places[i] > places[k]) & (places[i] < place_z), totals[i])
            for i in range(1, SIDE)
            if i != k
        )
        stage((refs[k], 0), log_decay, k - 1, keys, values)

    @pl.loop(0, SIDE - 1)
    def _(i):
        turn = jnp.where(i == 0, 3, i)
        is_before = (place_z + turn) % SIDE < place_z

        @pl.when(is_before)
        def _():
            attend(query_ref, keys, values, i * TOK, TOK, acc_ref)


def wanted(row):
    place_y = lax.axis_index("ctx") // SIDE
    return jnp.where(row == 0, place_y >= 1, place_y == SIDE - 1)


def first_body(query_ref, back_ref, ahead_ref, acc_ref, keys, values):
    zero = jnp.zeros((1, 1), F32)
    stage((back_ref, 0), zero, 0, keys, values)
    stage((ahead_ref, 0), zero, 1, keys, values)
    acc_ref[...] = jnp.zeros_like(acc_ref)

    @pl.loop(0, 2)
    def _(row):
        @pl.when(wanted(row))
        def _():
            attend(query_ref, keys, values, row * TOK, TOK, acc_ref.at[row])


def middle_body(query_ref, back0, back12, ahead0, ahead12, first_ref, acc_ref, keys, values):
    places = slot_places(lax.axis_index("ctx") % SIDE)
    later = [places[SIDE - 1] > places[k] for k in range(SIDE - 1)]
    for row, slots in enumerate(([(back0, 0), (back12, 0), (back12, 1)], [(ahead0, 0), (ahead12, 0), (ahead12, 1)])):
        totals = [total_of(*slot) for slot in slots]
        decays = [
            sum(gated(places[i] > places[k], totals[i]) for i in range(SIDE - 1) if i != k)
            for k in range(SIDE - 1)
        ]
        for k in (1, 2):
            stage(slots[k], decays[k], 2 * row + k - 1, keys, values)
        first = jnp.exp(decays[0]) * first_ref[row]
        acc_ref[row, 0] = gated(~later[0], first)
        acc_ref[row, 1] = gated(later[0], first)

    @pl.loop(0, 4)
    def _(i):
        row, slot = i // 2, 1 + i % 2
        group = jnp.where(slot == 1, later[1], later[2]).astype(jnp.int32)

        @pl.when(wanted(row))
        def _():
            attend(query_ref, keys, values, i * TOK, TOK, acc_ref.at[row, group])


def row_slots(first, middle, far):
    return [(first, 0), (middle, 0), (middle, 1), (far, 0)]


def near_body(
    query_ref, back0, back12, back3, ahead0, ahead12, ahead3, stat_ref, acc_in, groups,
    acc_ref, out_stat, keys, values
):
    places = slot_places(lax.axis_index("ctx") % SIDE)
    before = stat_ref[0:1, 0:1]
    for row, slots in enumerate((row_slots(back0, back12, back3), row_slots(ahead0, ahead12, ahead3))):
        totals = [total_of(*slot) for slot in slots]
        last = sum(gated(places[i] > places[SIDE - 1], totals[i]) for i in range(SIDE - 1))
        base = before if row == 0 else jnp.zeros_like(before)
        stage(slots[SIDE - 1], base + last, row, keys, values)
        both = jnp.exp(base) * groups[row, 0] + jnp.exp(base + totals[SIDE - 1]) * groups[row, 1]
        acc_ref[row] = acc_in[...] + both if row == 0 else both
        if row == 0:
            out_stat[...] = jnp.broadcast_to(before + sum(totals), out_stat.shape)

    @pl.loop(0, 2)
    def _(row):
        @pl.when(wanted(row))
        def _():
            attend(query_ref, keys, values, row * TOK, TOK, acc_ref.at[row])


def last_body(
    query_ref, far0, far12, far3, stat_ref, acc_in, own_ref, cum_ref, gain_ref,
    out_ref, acc, keys, values
):
    index = lax.axis_index("ctx")
    place_y, places = index // SIDE, slot_places(index % SIDE)
    before = stat_ref[0:1, 0:1]
    slots = row_slots(far0, far12, far3)
    totals = [total_of(*slot) for slot in slots]
    later = later_sums(places, totals)
    for k in range(SIDE):
        stage(slots[k], before + later[k], k, keys, values)
    acc[...] = acc_in[0]

    @pl.when(place_y == SIDE - 1)
    def _():
        acc[...] += jnp.exp(before + sum(totals)) * acc_in[1]

    @pl.when(place_y >= 2)
    def _():
        @pl.loop(0, 2)
        def _(i):
            attend(query_ref, keys, values, i * 2 * TOK, 2 * TOK, acc)

    grow = jnp.exp(column(cum_ref[...]))
    for head in range(GROUP_HEADS):
        cols = head_cols(head)
        number = own_ref[:, cols] + grow * acc[:, cols]
        mean = jnp.mean(number * number, axis=-1, keepdims=True)
        out_ref[:, cols] = (number * lax.rsqrt(mean + 1e-06) * gain_ref[0:1, cols]).astype(BF)


def features_of(weight_ref, step, flip):
    place = lax.axis_index("head")
    chunk = (place // 2 + step) % SIDE * 2 + (place % 2 + flip) % 2
    return weight_ref[:, pl.ds(pl.multiple_of(chunk * CHUNK, HEAD_DIM), CHUNK)]


def product(normed_ref, weight_ref, step, flip):
    return jnp.dot(
        normed_ref[...], features_of(weight_ref, step, flip), preferred_element_type=F32
    )


def other_far_body(normed_ref, weight_ref, out_ref):
    out_ref[...] = product(normed_ref, weight_ref, 2, 1).astype(BF)


def other_near_body(normed_ref, weight_ref, out_ref):
    @pl.loop(0, 3)
    def _(slot):
        step = jnp.where(slot == 0, 1, jnp.where(slot == 1, 3, 0))
        out_ref[slot] = product(normed_ref, weight_ref, step, 1).astype(BF)


def mine_far_body(normed_ref, weight_ref, other_ref, far_r, far_l):
    half = TOK // 2
    both = product(normed_ref, weight_ref, 2, 0) + other_ref[...].astype(F32)
    far_r[...] = both[:half].astype(BF)
    far_l[...] = both[half:].astype(BF)


def mine_near_body(normed_ref, weight_ref, other_ref, near_r, near_l, hold_r, hold_l, own_ref):
    half = TOK // 2
    both = product(normed_ref, weight_ref, 1, 0) + other_ref[0].astype(F32)
    hold_r[...] = both[:half]
    near_r[...] = both[half:].astype(BF)
    both = product(normed_ref, weight_ref, 3, 0) + other_ref[1].astype(F32)
    near_l[...] = both[:half].astype(BF)
    hold_l[...] = both[half:]
    own_ref[...] = product(normed_ref, weight_ref, 0, 0) + other_ref[2].astype(F32)


def pass_body(hold_r, far_r, hold_l, far_l, out_r, out_l):
    out_r[...] = (hold_r[...] + far_r[...].astype(F32)).astype(BF)
    out_l[...] = (hold_l[...] + far_l[...].astype(F32)).astype(BF)


def gather_body(own_ref, near_r, near_l, out_ref):
    half = TOK // 2
    out_ref[:half, :] = own_ref[:half, :] + near_l[...].astype(F32)
    out_ref[half:, :] = own_ref[half:, :] + near_r[...].astype(F32)


def finish_body(own_ref, sum_r, sum_l, out_ref):
    half = TOK // 2
    out_ref[:, :half] = (own_ref[:half, :] + sum_r[...].astype(F32)).T.astype(BF)
    out_ref[:, half:] = (own_ref[half:, :] + sum_l[...].astype(F32)).T.astype(BF)


def send(value, axis, pairs):
    return lax.ppermute(value, axis, pairs)


def per_device(queries, key_heads, value_heads, log_gates, norm_gain, out_weight):
    wide = GROUP_HEADS * HEAD_DIM
    after = lax.optimization_barrier
    payload, cum = kernel_call(
        prepare_body,
        (shape((PAY, 2 * HEAD_DIM), BF), shape((1, TOK), F32)),
        2**23,
        2**19,
        [pltpu.VMEM((TOK, HEAD_DIM), BF), pltpu.VMEM((1, TOK), F32), pltpu.SemaphoreType.DMA((3,))],
        in_specs=[pl.BlockSpec(memory_space=pltpu.HBM)] * 3,
    )(key_heads, value_heads, log_gates.reshape(1, TOK))
    row_back = send(payload, "ctx", CTX_Z[1])
    row_ahead = send(payload, "ctx", CTX_Z[-1])
    back0 = send(payload, "ctx", CTX_Y[1])
    ahead0 = send(payload, "ctx", CTX_Y[-1])
    block_flops = 4 * TOK * TOK * wide
    acc_shape, stat_shape = shape((TOK, wide), F32), shape((8, HEAD_DIM), F32)

    def scratch(blocks):
        return [pltpu.VMEM((blocks * TOK, HEAD_DIM), BF)] * 2

    own = kernel_call(own_body, acc_shape, block_flops, 2**21, in_specs=[VMEM] * 4)(
        queries, key_heads, value_heads, cum
    )
    row_far = send(row_back, "ctx", CTX_Z[1])
    middle = jnp.concatenate([row_back, row_ahead], axis=0)
    middle, own = after((middle, own))
    back12 = send(middle, "ctx", CTX_Y[1])
    ahead12 = send(middle, "ctx", CTX_Y[-1])
    first = kernel_call(
        first_body, shape((2, TOK, wide), F32), 2 * block_flops, 2**21, scratch(2), in_specs=[VMEM] * 3
    )(queries, back0, ahead0)
    acc, stat = kernel_call(
        row_body, (acc_shape, stat_shape), 3 * block_flops, 2**21, scratch(3), in_specs=[VMEM] * 5
    )(queries, payload, row_back, row_ahead, row_far)
    pass_back, pass_ahead, pass0, pass_far, acc, first = after(
        (back12, ahead12, ahead0, row_far, acc, first)
    )
    far12 = send(pass_back, "ctx", CTX_Y[1])
    far0 = send(pass0, "ctx", CTX_Y[-1])
    back3 = send(pass_back[PAY:], "ctx", CTX_Z[-1])
    ahead3 = send(pass_ahead[:PAY], "ctx", CTX_Z[1])
    far3 = send(pass_far, "ctx", CTX_Y[2])
    groups = kernel_call(
        middle_body,
        shape((2, 2, TOK, wide), F32),
        24 * block_flops,
        2**22,
        scratch(4),
        in_specs=[VMEM] * 6,
    )(queries, back0, back12, ahead0, ahead12, first)
    acc, stat = kernel_call(
        near_body,
        (shape((2, TOK, wide), F32), stat_shape),
        2 * block_flops,
        2**22,
        scratch(2),
        in_specs=[VMEM] * 10,
    )(queries, back0, back12, back3, ahead0, ahead12, ahead3, stat, acc, groups)
    normed = kernel_call(
        last_body,
        shape((TOK, wide), BF),
        4 * block_flops,
        2**22,
        [pltpu.VMEM((TOK, wide), F32), *scratch(4)],
        in_specs=[VMEM] * 9,
    )(queries, far0, far12, far3, stat, acc, own, cum, norm_gain.reshape(1, wide))

    chunk_flops = 2 * TOK * CHUNK * wide
    chunk = shape((TOK, CHUNK), BF)
    half_bf, half_f32 = shape((TOK // 2, CHUNK), BF), shape((TOK // 2, CHUNK), F32)
    other_far = kernel_call(other_far_body, chunk, chunk_flops, 2**20, in_specs=[VMEM] * 2)(
        normed, out_weight
    )
    normed, other_far = after((normed, other_far))
    other_far = send(other_far, "head", CORE)
    other_near = kernel_call(
        other_near_body, shape((3, TOK, CHUNK), BF), 30 * chunk_flops, 2**21, in_specs=[VMEM] * 2
    )(normed, out_weight)
    other_near = send(other_near, "head", CORE)
    far_r, far_l = kernel_call(
        mine_far_body, (half_bf, half_bf), 30 * chunk_flops, 2**20, in_specs=[VMEM] * 3
    )(normed, out_weight, other_far)
    far_r = send(far_r, "head", HEAD_X[1])
    far_l = send(far_l, "head", HEAD_X[-1])
    near_r, near_l, hold_r, hold_l, own_sum = kernel_call(
        mine_near_body,
        (half_bf, half_bf, half_f32, half_f32, shape((TOK, CHUNK), F32)),
        3 * chunk_flops,
        2**22,
        in_specs=[VMEM] * 3,
    )(normed, out_weight, other_near)
    near_r = send(near_r, "head", HEAD_X[1])
    near_l = send(near_l, "head", HEAD_X[-1])
    sum_r, sum_l = kernel_call(pass_body, (half_bf,) * 2, 2**19, 2**21, in_specs=[VMEM] * 4)(
        hold_r, far_r, hold_l, far_l
    )
    sum_r = send(sum_r, "head", HEAD_X[1])
    sum_l = send(sum_l, "head", HEAD_X[-1])
    own_sum = kernel_call(
        gather_body, shape((TOK, CHUNK), F32), 2**20, 2**22, in_specs=[VMEM] * 3
    )(own_sum, near_r, near_l)
    return kernel_call(finish_body, shape((CHUNK, TOK), BF), 2**20, 2**22, in_specs=[VMEM] * 3)(
        own_sum, sum_r, sum_l
    )


def solution(mesh):
    return jax.shard_map(
        per_device,
        mesh=mesh,
        in_specs=(
            P("ctx", "head"),
            P("ctx", "head"),
            P("ctx", "head"),
            P("ctx", "head"),
            P("head"),
            P("head", None),
        ),
        out_specs=P("head", "ctx"),
        check_vma=False,
    )
```

```python
import jax
import jax.numpy as jnp
from jax import lax
from jax.experimental import pallas as pl
from jax.experimental.pallas import tpu as pltpu
from jax.sharding import PartitionSpec as P

HEAD_DIM = 128
GROUP_HEADS = 5
TOK = 512
PAY = TOK + 16
SIDE = 4
CHUNK = 640
BF = jnp.bfloat16
F32 = jnp.float32
VMEM = pl.BlockSpec(memory_space=pltpu.VMEM)

CTX = SIDE * SIDE
CTX_Z = {d: [(i, (i // SIDE) * SIDE + (i + d) % SIDE) for i in range(CTX)] for d in (1, -1)}
CTX_Y = {d: [(i, (i + d * SIDE) % CTX) for i in range(CTX)] for d in (1, -1, 2)}
HEAD_X = {d: [(i, (i + 2 * d) % (2 * SIDE)) for i in range(2 * SIDE)] for d in (1, -1)}
CORE = [(i, i ^ 1) for i in range(2 * SIDE)]


def kernel_call(body, outs, flops, nbytes, scratch=(), vmem=24 * 2**20, **extra):
    return pl.pallas_call(
        body,
        out_shape=outs,
        in_specs=extra.pop("in_specs"),
        out_specs=extra.pop("out_specs", jax.tree.map(lambda _: VMEM, outs)),
        scratch_shapes=list(scratch),
        compiler_params=pltpu.CompilerParams(vmem_limit_bytes=vmem),
        cost_estimate=pl.CostEstimate(flops=flops, bytes_accessed=nbytes, transcendentals=0),
        **extra,
    )


def shape(dims, kind):
    return jax.ShapeDtypeStruct(dims, kind)


def column(row):
    return jnp.broadcast_to(row, (HEAD_DIM, TOK)).T[:, :1]


def prepare_body(key_hbm, value_hbm, gate_hbm, out_ref, cum_ref, value_ref, gate_ref, sems):
    copies = [
        pltpu.make_async_copy(gate_hbm, gate_ref, sems.at[0]),
        pltpu.make_async_copy(value_hbm, value_ref, sems.at[1]),
        pltpu.make_async_copy(key_hbm, out_ref.at[pl.ds(0, TOK), pl.ds(0, HEAD_DIM)], sems.at[2]),
    ]
    for copy in copies:
        copy.start()
    copies[0].wait()
    gates = gate_ref[...]
    top = gates.astype(BF).astype(F32)
    mid = (gates - top).astype(BF).astype(F32)
    rows = lax.broadcasted_iota(jnp.int32, (16, TOK), 0)
    parts = jnp.where(rows == 0, top, jnp.where(rows == 1, mid, gates - top - mid))
    parts = jnp.where(rows < 3, parts, 0.0).astype(BF)
    source = lax.broadcasted_iota(jnp.int32, (TOK, TOK), 0)
    place = lax.broadcasted_iota(jnp.int32, (TOK, TOK), 1)
    upto = jnp.where(source <= place, 1.0, 0.0).astype(BF)
    sums = jnp.dot(parts, upto, preferred_element_type=F32)
    cum = jnp.sum(sums, axis=0, keepdims=True)
    cum_ref[...] = cum
    total = cum[:, TOK - 1 :]
    copies[1].wait()
    out_ref[:TOK, HEAD_DIM:] = (value_ref[...].astype(F32) * jnp.exp(total - column(cum))).astype(BF)
    top = total.astype(BF).astype(F32)
    mid = (total - top).astype(BF).astype(F32)
    rows = lax.broadcasted_iota(jnp.int32, (16, HEAD_DIM), 0)
    lanes = lax.broadcasted_iota(jnp.int32, (16, HEAD_DIM), 1)
    tile = jnp.where(lanes == 0, top, jnp.where(lanes == 1, mid, jnp.where(lanes == 2, total - top - mid, 0.0)))
    out_ref[TOK:, :HEAD_DIM] = jnp.where(rows == 0, tile, 0.0).astype(BF)
    out_ref[TOK:, HEAD_DIM:] = jnp.zeros((16, HEAD_DIM), BF)
    copies[2].wait()


def inner(query, key):
    return lax.dot_general(query, key, (((1,), (1,)), ((), ())), preferred_element_type=F32)


def head_cols(head):
    return slice(head * HEAD_DIM, (head + 1) * HEAD_DIM)


def own_body(query_ref, key_ref, value_ref, cum_ref, out_ref):
    cum_col = column(cum_ref[...])
    half = TOK // 2
    for part in range(2):
        rows = slice(part * half, (part + 1) * half)
        seen = (part + 1) * half
        place = part * half + lax.broadcasted_iota(jnp.int32, (half, seen), 0)
        source = lax.broadcasted_iota(jnp.int32, (half, seen), 1)
        decay = jnp.exp(jnp.minimum(cum_col[rows] - cum_ref[0:1, :seen], 0.0))
        decay = jnp.where(place >= source, decay, 0.0)
        for head in range(GROUP_HEADS):
            scores = inner(query_ref[rows, head_cols(head)], key_ref[:seen, :])
            scores = (scores * scores * decay).astype(BF)
            out_ref[rows, head_cols(head)] = jnp.dot(
                scores, value_ref[:seen, :], preferred_element_type=F32
            )


def total_of(ref, slot):
    tile = ref[slot * PAY + TOK : (slot + 1) * PAY, :HEAD_DIM].astype(F32)
    return jnp.sum(jnp.sum(tile, axis=1, keepdims=True), axis=0, keepdims=True)


def slot_places(place_z):
    return [place_z, (place_z + 3) % SIDE, (place_z + 1) % SIDE, (place_z + 2) % SIDE]


def gated(condition, value):
    return jnp.where(condition, value, jnp.zeros_like(value))


def later_sums(places, totals):
    return [
        sum(gated(places[i] > places[k], totals[i]) for i in range(SIDE) if i != k)
        for k in range(SIDE)
    ]


def stage(slot, log_decay, place, keys, values):
    ref, index = slot
    rows = slice(index * PAY, index * PAY + TOK)
    target = slice(place * TOK, (place + 1) * TOK)
    keys[target, :] = ref[rows, :HEAD_DIM]
    values[target, :] = (ref[rows, HEAD_DIM:].astype(F32) * jnp.exp(log_decay)).astype(BF)


def attend(query_ref, keys, values, start, size, acc_ref):
    rows = pl.ds(pl.multiple_of(start, size), size)
    key, value = keys[rows, :], values[rows, :]
    for head in range(GROUP_HEADS):
        scores = inner(query_ref[:, head_cols(head)], key)
        scores = (scores * scores).astype(BF)
        acc_ref[:, head_cols(head)] += jnp.dot(scores, value, preferred_element_type=F32)


def row_body(query_ref, own_ref, back_ref, ahead_ref, far_ref, acc_ref, stat_ref, keys, values):
    place_z = lax.axis_index("ctx") % SIDE
    places = slot_places(place_z)
    refs = [own_ref, back_ref, ahead_ref, far_ref]
    totals = [total_of(ref, 0) for ref in refs]
    acc_ref[...] = jnp.zeros_like(acc_ref)
    before = sum(gated(places[k] < place_z, totals[k]) for k in range(1, SIDE))
    stat_ref[...] = jnp.broadcast_to(before, stat_ref.shape)
    for k in range(1, SIDE):
        log_decay = sum(
            gated((places[i] > places[k]) & (places[i] < place_z), totals[i])
            for i in range(1, SIDE)
            if i != k
        )
        stage((refs[k], 0), log_decay, k - 1, keys, values)

    @pl.loop(0, SIDE - 1)
    def _(i):
        turn = jnp.where(i == 0, 3, i)
        is_before = (place_z + turn) % SIDE < place_z

        @pl.when(is_before)
        def _():
            attend(query_ref, keys, values, i * TOK, TOK, acc_ref)


def wanted(row):
    place_y = lax.axis_index("ctx") // SIDE
    return jnp.where(row == 0, place_y >= 1, place_y == SIDE - 1)


def first_body(query_ref, back_ref, ahead_ref, acc_ref, keys, values):
    zero = jnp.zeros((1, 1), F32)
    stage((back_ref, 0), zero, 0, keys, values)
    stage((ahead_ref, 0), zero, 1, keys, values)
    acc_ref[...] = jnp.zeros_like(acc_ref)

    @pl.loop(0, 2)
    def _(row):
        @pl.when(wanted(row))
        def _():
            attend(query_ref, keys, values, row * TOK, TOK, acc_ref.at[row])


def middle_body(query_ref, back0, back12, ahead0, ahead12, first_ref, acc_ref, keys, values):
    places = slot_places(lax.axis_index("ctx") % SIDE)
    later = [places[SIDE - 1] > places[k] for k in range(SIDE - 1)]
    for row, slots in enumerate(([(back0, 0), (back12, 0), (back12, 1)], [(ahead0, 0), (ahead12, 0), (ahead12, 1)])):
        totals = [total_of(*slot) for slot in slots]
        decays = [
            sum(gated(places[i] > places[k], totals[i]) for i in range(SIDE - 1) if i != k)
            for k in range(SIDE - 1)
        ]
        for k in (1, 2):
            stage(slots[k], decays[k], 2 * row + k - 1, keys, values)
        first = jnp.exp(decays[0]) * first_ref[row]
        acc_ref[row, 0] = gated(~later[0], first)
        acc_ref[row, 1] = gated(later[0], first)

    @pl.loop(0, 4)
    def _(i):
        row, slot = i // 2, 1 + i % 2
        group = jnp.where(slot == 1, later[1], later[2]).astype(jnp.int32)

        @pl.when(wanted(row))
        def _():
            attend(query_ref, keys, values, i * TOK, TOK, acc_ref.at[row, group])


def row_slots(first, middle, far):
    return [(first, 0), (middle, 0), (middle, 1), (far, 0)]


def near_body(
    query_ref, back0, back12, back3, ahead0, ahead12, ahead3, stat_ref, acc_in, groups,
    acc_ref, out_stat, keys, values
):
    places = slot_places(lax.axis_index("ctx") % SIDE)
    before = stat_ref[0:1, 0:1]
    for row, slots in enumerate((row_slots(back0, back12, back3), row_slots(ahead0, ahead12, ahead3))):
        totals = [total_of(*slot) for slot in slots]
        last = sum(gated(places[i] > places[SIDE - 1], totals[i]) for i in range(SIDE - 1))
        base = before if row == 0 else jnp.zeros_like(before)
        stage(slots[SIDE - 1], base + last, row, keys, values)
        both = jnp.exp(base) * groups[row, 0] + jnp.exp(base + totals[SIDE - 1]) * groups[row, 1]
        acc_ref[row] = acc_in[...] + both if row == 0 else both
        if row == 0:
            out_stat[...] = jnp.broadcast_to(before + sum(totals), out_stat.shape)

    @pl.loop(0, 2)
    def _(row):
        @pl.when(wanted(row))
        def _():
            attend(query_ref, keys, values, row * TOK, TOK, acc_ref.at[row])


def last_body(
    query_ref, far0, far12, far3, stat_ref, acc_in, own_ref, cum_ref, gain_ref,
    out_ref, acc, keys, values
):
    index = lax.axis_index("ctx")
    place_y, places = index // SIDE, slot_places(index % SIDE)
    before = stat_ref[0:1, 0:1]
    slots = row_slots(far0, far12, far3)
    totals = [total_of(*slot) for slot in slots]
    later = later_sums(places, totals)
    for k in range(SIDE):
        stage(slots[k], before + later[k], k, keys, values)
    acc[...] = acc_in[0]

    @pl.when(place_y == SIDE - 1)
    def _():
        acc[...] += jnp.exp(before + sum(totals)) * acc_in[1]

    @pl.when(place_y >= 2)
    def _():
        @pl.loop(0, 2)
        def _(i):
            attend(query_ref, keys, values, i * 2 * TOK, 2 * TOK, acc)

    grow = jnp.exp(column(cum_ref[...]))
    for head in range(GROUP_HEADS):
        cols = head_cols(head)
        number = own_ref[:, cols] + grow * acc[:, cols]
        mean = jnp.mean(number * number, axis=-1, keepdims=True)
        out_ref[:, cols] = (number * lax.rsqrt(mean + 1e-06) * gain_ref[0:1, cols]).astype(BF)


def features_of(weight_ref, step, flip):
    place = lax.axis_index("head")
    chunk = (place // 2 + step) % SIDE * 2 + (place % 2 + flip) % 2
    return weight_ref[:, pl.ds(pl.multiple_of(chunk * CHUNK, HEAD_DIM), CHUNK)]


def product(normed_ref, weight_ref, step, flip):
    return jnp.dot(
        normed_ref[...], features_of(weight_ref, step, flip), preferred_element_type=F32
    )


def other_far_body(normed_ref, weight_ref, out_ref):
    out_ref[...] = product(normed_ref, weight_ref, 2, 1).astype(BF)


def other_near_body(normed_ref, weight_ref, out_ref):
    @pl.loop(0, 3)
    def _(slot):
        step = jnp.where(slot == 0, 1, jnp.where(slot == 1, 3, 0))
        out_ref[slot] = product(normed_ref, weight_ref, step, 1).astype(BF)


def mine_far_body(normed_ref, weight_ref, other_ref, far_r, far_l):
    half = TOK // 2
    both = product(normed_ref, weight_ref, 2, 0) + other_ref[...].astype(F32)
    far_r[...] = both[:half].astype(BF)
    far_l[...] = both[half:].astype(BF)


def mine_near_body(normed_ref, weight_ref, other_ref, near_r, near_l, hold_r, hold_l, own_ref):
    half = TOK // 2
    both = product(normed_ref, weight_ref, 1, 0) + other_ref[0].astype(F32)
    hold_r[...] = both[:half]
    near_r[...] = both[half:].astype(BF)
    both = product(normed_ref, weight_ref, 3, 0) + other_ref[1].astype(F32)
    near_l[...] = both[:half].astype(BF)
    hold_l[...] = both[half:]
    own_ref[...] = product(normed_ref, weight_ref, 0, 0) + other_ref[2].astype(F32)


def pass_body(hold_r, far_r, hold_l, far_l, out_r, out_l):
    out_r[...] = (hold_r[...] + far_r[...].astype(F32)).astype(BF)
    out_l[...] = (hold_l[...] + far_l[...].astype(F32)).astype(BF)


def gather_body(own_ref, near_r, near_l, out_ref):
    half = TOK // 2
    out_ref[:half, :] = own_ref[:half, :] + near_l[...].astype(F32)
    out_ref[half:, :] = own_ref[half:, :] + near_r[...].astype(F32)


def finish_body(own_ref, sum_r, sum_l, out_ref):
    half = TOK // 2
    out_ref[:, :half] = (own_ref[:half, :] + sum_r[...].astype(F32)).T.astype(BF)
    out_ref[:, half:] = (own_ref[half:, :] + sum_l[...].astype(F32)).T.astype(BF)


def send(value, axis, pairs):
    return lax.ppermute(value, axis, pairs)


def per_device(queries, key_heads, value_heads, log_gates, norm_gain, out_weight):
    wide = GROUP_HEADS * HEAD_DIM
    after = lax.optimization_barrier
    payload, cum = kernel_call(
        prepare_body,
        (shape((PAY, 2 * HEAD_DIM), BF), shape((1, TOK), F32)),
        2**23,
        2**19,
        [pltpu.VMEM((TOK, HEAD_DIM), BF), pltpu.VMEM((1, TOK), F32), pltpu.SemaphoreType.DMA((3,))],
        vmem=60 * 2**20,
        in_specs=[pl.BlockSpec(memory_space=pltpu.HBM)] * 3,
    )(key_heads, value_heads, log_gates.reshape(1, TOK))
    row_back = send(payload, "ctx", CTX_Z[1])
    row_ahead = send(payload, "ctx", CTX_Z[-1])
    back0 = send(payload, "ctx", CTX_Y[1])
    ahead0 = send(payload, "ctx", CTX_Y[-1])
    block_flops = 4 * TOK * TOK * wide
    acc_shape, stat_shape = shape((TOK, wide), F32), shape((8, HEAD_DIM), F32)

    def scratch(blocks):
        return [pltpu.VMEM((blocks * TOK, HEAD_DIM), BF)] * 2

    row_far = send(row_back, "ctx", CTX_Z[1])
    middle = jnp.concatenate([row_back, row_ahead], axis=0)
    middle, own_keys = after((middle, key_heads))
    own = kernel_call(own_body, acc_shape, 8 * block_flops, 2**21, in_specs=[VMEM] * 4)(
        queries, own_keys, value_heads, cum
    )
    first0, own = after((back0, own))
    back12 = send(middle, "ctx", CTX_Y[1])
    ahead12 = send(middle, "ctx", CTX_Y[-1])
    first = kernel_call(
        first_body, shape((2, TOK, wide), F32), 2 * block_flops, 2**21, scratch(2), in_specs=[VMEM] * 3
    )(queries, first0, ahead0)
    pass0, row_far, first = after((ahead0, row_far, first))
    far0 = send(pass0, "ctx", CTX_Y[-1])
    acc, stat = kernel_call(
        row_body, (acc_shape, stat_shape), 24 * block_flops, 2**21, scratch(3), in_specs=[VMEM] * 5
    )(queries, payload, row_back, row_ahead, row_far)
    pass_back, pass_far, acc = after((back12, row_far, acc))
    far12 = send(pass_back, "ctx", CTX_Y[1])
    back3 = send(pass_back[PAY:], "ctx", CTX_Z[-1])
    far3 = send(pass_far, "ctx", CTX_Y[2])
    ahead3 = send(ahead12[:PAY], "ctx", CTX_Z[1])
    groups = kernel_call(
        middle_body,
        shape((2, 2, TOK, wide), F32),
        24 * block_flops,
        2**22,
        scratch(4),
        in_specs=[VMEM] * 6,
    )(queries, back0, back12, ahead0, ahead12, first)
    acc, stat = kernel_call(
        near_body,
        (shape((2, TOK, wide), F32), stat_shape),
        2 * block_flops,
        2**22,
        scratch(2),
        in_specs=[VMEM] * 10,
    )(queries, back0, back12, back3, ahead0, ahead12, ahead3, stat, acc, groups)
    normed = kernel_call(
        last_body,
        shape((TOK, wide), BF),
        4 * block_flops,
        2**22,
        [pltpu.VMEM((TOK, wide), F32), *scratch(4)],
        in_specs=[VMEM] * 9,
    )(queries, far0, far12, far3, stat, acc, own, cum, norm_gain.reshape(1, wide))

    chunk_flops = 2 * TOK * CHUNK * wide
    chunk = shape((TOK, CHUNK), BF)
    half_bf, half_f32 = shape((TOK // 2, CHUNK), BF), shape((TOK // 2, CHUNK), F32)
    other_far = kernel_call(other_far_body, chunk, chunk_flops, 2**20, in_specs=[VMEM] * 2)(
        normed, out_weight
    )
    normed, other_far = after((normed, other_far))
    other_far = send(other_far, "head", CORE)
    other_near = kernel_call(
        other_near_body, shape((3, TOK, CHUNK), BF), 30 * chunk_flops, 2**21, in_specs=[VMEM] * 2
    )(normed, out_weight)
    other_near = send(other_near, "head", CORE)
    far_r, far_l = kernel_call(
        mine_far_body, (half_bf, half_bf), 30 * chunk_flops, 2**20, in_specs=[VMEM] * 3
    )(normed, out_weight, other_far)
    far_r = send(far_r, "head", HEAD_X[1])
    far_l = send(far_l, "head", HEAD_X[-1])
    near_r, near_l, hold_r, hold_l, own_sum = kernel_call(
        mine_near_body,
        (half_bf, half_bf, half_f32, half_f32, shape((TOK, CHUNK), F32)),
        3 * chunk_flops,
        2**22,
        in_specs=[VMEM] * 3,
    )(normed, out_weight, other_near)
    near_r = send(near_r, "head", HEAD_X[1])
    near_l = send(near_l, "head", HEAD_X[-1])
    sum_r, sum_l = kernel_call(pass_body, (half_bf,) * 2, 2**19, 2**21, in_specs=[VMEM] * 4)(
        hold_r, far_r, hold_l, far_l
    )
    sum_r = send(sum_r, "head", HEAD_X[1])
    sum_l = send(sum_l, "head", HEAD_X[-1])
    own_sum = kernel_call(
        gather_body, shape((TOK, CHUNK), F32), 2**20, 2**22, in_specs=[VMEM] * 3
    )(own_sum, near_r, near_l)
    return kernel_call(finish_body, shape((CHUNK, TOK), BF), 2**20, 2**22, in_specs=[VMEM] * 3)(
        own_sum, sum_r, sum_l
    )


def solution(mesh):
    return jax.shard_map(
        per_device,
        mesh=mesh,
        in_specs=(
            P("ctx", "head"),
            P("ctx", "head"),
            P("ctx", "head"),
            P("ctx", "head"),
            P("head"),
            P("head", None),
        ),
        out_specs=P("head", "ctx"),
        check_vma=False,
    )
```

```python
import jax
import jax.numpy as jnp
from jax import lax
from jax.experimental import pallas as pl
from jax.experimental.pallas import tpu as pltpu
from jax.sharding import PartitionSpec as P

HEAD_DIM = 128
GROUP_HEADS = 5
TOK = 512
PAY = TOK + 16
SIDE = 4
CHUNK = 640
SPLIT = TOK // 2
BF = jnp.bfloat16
F32 = jnp.float32
VMEM = pl.BlockSpec(memory_space=pltpu.VMEM)

CTX = SIDE * SIDE
CTX_Z = {d: [(i, (i // SIDE) * SIDE + (i + d) % SIDE) for i in range(CTX)] for d in (1, -1)}
CTX_Y = {d: [(i, (i + d * SIDE) % CTX) for i in range(CTX)] for d in (1, -1, 2)}
HEAD_X = {d: [(i, (i + 2 * d) % (2 * SIDE)) for i in range(2 * SIDE)] for d in (1, -1)}
CORE = [(i, i ^ 1) for i in range(2 * SIDE)]


def kernel_call(body, outs, flops, nbytes, scratch=(), vmem=24 * 2**20, **extra):
    return pl.pallas_call(
        body,
        out_shape=outs,
        in_specs=extra.pop("in_specs"),
        out_specs=extra.pop("out_specs", jax.tree.map(lambda _: VMEM, outs)),
        scratch_shapes=list(scratch),
        compiler_params=pltpu.CompilerParams(vmem_limit_bytes=vmem),
        cost_estimate=pl.CostEstimate(flops=flops, bytes_accessed=nbytes, transcendentals=0),
        **extra,
    )


def shape(dims, kind):
    return jax.ShapeDtypeStruct(dims, kind)


def column(row):
    return jnp.broadcast_to(row, (HEAD_DIM, TOK)).T[:, :1]


def prepare_body(key_hbm, value_hbm, gate_hbm, out_ref, cum_ref, value_ref, gate_ref, sems):
    copies = [
        pltpu.make_async_copy(gate_hbm, gate_ref, sems.at[0]),
        pltpu.make_async_copy(value_hbm, value_ref, sems.at[1]),
        pltpu.make_async_copy(key_hbm, out_ref.at[pl.ds(0, TOK), pl.ds(0, HEAD_DIM)], sems.at[2]),
    ]
    for copy in copies:
        copy.start()
    copies[0].wait()
    gates = gate_ref[...]
    top = gates.astype(BF).astype(F32)
    mid = (gates - top).astype(BF).astype(F32)
    rows = lax.broadcasted_iota(jnp.int32, (16, TOK), 0)
    parts = jnp.where(rows == 0, top, jnp.where(rows == 1, mid, gates - top - mid))
    parts = jnp.where(rows < 3, parts, 0.0).astype(BF)
    source = lax.broadcasted_iota(jnp.int32, (TOK, TOK), 0)
    place = lax.broadcasted_iota(jnp.int32, (TOK, TOK), 1)
    upto = jnp.where(source <= place, 1.0, 0.0).astype(BF)
    sums = jnp.dot(parts, upto, preferred_element_type=F32)
    cum = jnp.sum(sums, axis=0, keepdims=True)
    cum_ref[...] = cum
    total = cum[:, TOK - 1 :]
    copies[1].wait()
    out_ref[:TOK, HEAD_DIM:] = (value_ref[...].astype(F32) * jnp.exp(total - column(cum))).astype(BF)
    top = total.astype(BF).astype(F32)
    mid = (total - top).astype(BF).astype(F32)
    rows = lax.broadcasted_iota(jnp.int32, (16, HEAD_DIM), 0)
    lanes = lax.broadcasted_iota(jnp.int32, (16, HEAD_DIM), 1)
    tile = jnp.where(lanes == 0, top, jnp.where(lanes == 1, mid, jnp.where(lanes == 2, total - top - mid, 0.0)))
    out_ref[TOK:, :HEAD_DIM] = jnp.where(rows == 0, tile, 0.0).astype(BF)
    out_ref[TOK:, HEAD_DIM:] = jnp.zeros((16, HEAD_DIM), BF)
    copies[2].wait()


def inner(query, key):
    return lax.dot_general(query, key, (((1,), (1,)), ((), ())), preferred_element_type=F32)


def head_cols(head):
    return slice(head * HEAD_DIM, (head + 1) * HEAD_DIM)


def own_body(query_ref, key_ref, value_ref, cum_ref, out_ref):
    cum_col = column(cum_ref[...])
    half = TOK // 2
    for part in range(2):
        rows = slice(part * half, (part + 1) * half)
        seen = (part + 1) * half
        place = part * half + lax.broadcasted_iota(jnp.int32, (half, seen), 0)
        source = lax.broadcasted_iota(jnp.int32, (half, seen), 1)
        decay = jnp.exp(jnp.minimum(cum_col[rows] - cum_ref[0:1, :seen], 0.0))
        decay = jnp.where(place >= source, decay, 0.0)
        for head in range(GROUP_HEADS):
            scores = inner(query_ref[rows, head_cols(head)], key_ref[:seen, :])
            scores = (scores * scores * decay).astype(BF)
            out_ref[rows, head_cols(head)] = jnp.dot(
                scores, value_ref[:seen, :], preferred_element_type=F32
            )


def total_of(ref, slot):
    tile = ref[slot * PAY + TOK : (slot + 1) * PAY, :HEAD_DIM].astype(F32)
    return jnp.sum(jnp.sum(tile, axis=1, keepdims=True), axis=0, keepdims=True)


def slot_places(place_z):
    return [place_z, (place_z + 3) % SIDE, (place_z + 1) % SIDE, (place_z + 2) % SIDE]


def gated(condition, value):
    return jnp.where(condition, value, jnp.zeros_like(value))


def later_sums(places, totals):
    return [
        sum(gated(places[i] > places[k], totals[i]) for i in range(SIDE) if i != k)
        for k in range(SIDE)
    ]


def stage(slot, log_decay, place, keys, values):
    ref, index = slot
    rows = slice(index * PAY, index * PAY + TOK)
    target = slice(place * TOK, (place + 1) * TOK)
    keys[target, :] = ref[rows, :HEAD_DIM]
    values[target, :] = (ref[rows, HEAD_DIM:].astype(F32) * jnp.exp(log_decay)).astype(BF)


def attend(query_ref, keys, values, start, size, acc_ref):
    rows = pl.ds(pl.multiple_of(start, size), size)
    key, value = keys[rows, :], values[rows, :]
    for head in range(GROUP_HEADS):
        scores = inner(query_ref[:, head_cols(head)], key)
        scores = (scores * scores).astype(BF)
        acc_ref[:, head_cols(head)] += jnp.dot(scores, value, preferred_element_type=F32)


def row_body(query_ref, own_ref, back_ref, ahead_ref, far_ref, acc_ref, stat_ref, keys, values):
    place_z = lax.axis_index("ctx") % SIDE
    places = slot_places(place_z)
    refs = [own_ref, back_ref, ahead_ref, far_ref]
    totals = [total_of(ref, 0) for ref in refs]
    acc_ref[...] = jnp.zeros_like(acc_ref)
    before = sum(gated(places[k] < place_z, totals[k]) for k in range(1, SIDE))
    stat_ref[...] = jnp.broadcast_to(before, stat_ref.shape)
    for k in range(1, SIDE):
        log_decay = sum(
            gated((places[i] > places[k]) & (places[i] < place_z), totals[i])
            for i in range(1, SIDE)
            if i != k
        )
        stage((refs[k], 0), log_decay, k - 1, keys, values)

    @pl.loop(0, SIDE - 1)
    def _(i):
        turn = jnp.where(i == 0, 3, i)
        is_before = (place_z + turn) % SIDE < place_z

        @pl.when(is_before)
        def _():
            attend(query_ref, keys, values, i * TOK, TOK, acc_ref)


def wanted(row):
    place_y = lax.axis_index("ctx") // SIDE
    return jnp.where(row == 0, place_y >= 1, place_y == SIDE - 1)


def first_body(query_ref, back_ref, ahead_ref, acc_ref, keys, values):
    zero = jnp.zeros((1, 1), F32)
    stage((back_ref, 0), zero, 0, keys, values)
    stage((ahead_ref, 0), zero, 1, keys, values)
    acc_ref[...] = jnp.zeros_like(acc_ref)

    @pl.loop(0, 2)
    def _(row):
        @pl.when(wanted(row))
        def _():
            attend(query_ref, keys, values, row * TOK, TOK, acc_ref.at[row])


def middle_body(query_ref, back0, back12, ahead0, ahead12, first_ref, acc_ref, keys, values):
    places = slot_places(lax.axis_index("ctx") % SIDE)
    later = [places[SIDE - 1] > places[k] for k in range(SIDE - 1)]
    for row, slots in enumerate(([(back0, 0), (back12, 0), (back12, 1)], [(ahead0, 0), (ahead12, 0), (ahead12, 1)])):
        totals = [total_of(*slot) for slot in slots]
        decays = [
            sum(gated(places[i] > places[k], totals[i]) for i in range(SIDE - 1) if i != k)
            for k in range(SIDE - 1)
        ]
        for k in (1, 2):
            stage(slots[k], decays[k], 2 * row + k - 1, keys, values)
        first = jnp.exp(decays[0]) * first_ref[row]
        acc_ref[row, 0] = gated(~later[0], first)
        acc_ref[row, 1] = gated(later[0], first)

    @pl.loop(0, 4)
    def _(i):
        row, slot = i // 2, 1 + i % 2
        group = jnp.where(slot == 1, later[1], later[2]).astype(jnp.int32)

        @pl.when(wanted(row))
        def _():
            attend(query_ref, keys, values, i * TOK, TOK, acc_ref.at[row, group])


def row_slots(first, middle, far):
    return [(first, 0), (middle, 0), (middle, 1), (far, 0)]


def near_body(
    query_ref, back0, back12, back3, ahead0, ahead12, ahead3, stat_ref, acc_in, groups,
    acc_ref, out_stat, keys, values
):
    places = slot_places(lax.axis_index("ctx") % SIDE)
    before = stat_ref[0:1, 0:1]
    for row, slots in enumerate((row_slots(back0, back12, back3), row_slots(ahead0, ahead12, ahead3))):
        totals = [total_of(*slot) for slot in slots]
        last = sum(gated(places[i] > places[SIDE - 1], totals[i]) for i in range(SIDE - 1))
        base = before if row == 0 else jnp.zeros_like(before)
        stage(slots[SIDE - 1], base + last, row, keys, values)
        both = jnp.exp(base) * groups[row, 0] + jnp.exp(base + totals[SIDE - 1]) * groups[row, 1]
        acc_ref[row] = acc_in[...] + both if row == 0 else both
        if row == 0:
            out_stat[...] = jnp.broadcast_to(before + sum(totals), out_stat.shape)

    @pl.loop(0, 2)
    def _(row):
        @pl.when(wanted(row))
        def _():
            attend(query_ref, keys, values, row * TOK, TOK, acc_ref.at[row])


def last_body(
    query_ref, far0, far12, far3, stat_ref, acc_in, own_ref, cum_ref, gain_ref, weight_ref,
    out_ref, other_ref, acc, keys, values
):
    index = lax.axis_index("ctx")
    place_y, places = index // SIDE, slot_places(index % SIDE)
    before = stat_ref[0:1, 0:1]
    slots = row_slots(far0, far12, far3)
    totals = [total_of(*slot) for slot in slots]
    later = later_sums(places, totals)
    for k in range(SIDE):
        stage(slots[k], before + later[k], k, keys, values)
    acc[...] = acc_in[0]

    @pl.when(place_y == SIDE - 1)
    def _():
        acc[...] += jnp.exp(before + sum(totals)) * acc_in[1]

    @pl.when(place_y >= 2)
    def _():
        attend(query_ref, keys, values, 0, SIDE * TOK, acc)

    grow = jnp.exp(column(cum_ref[...]))
    for head in range(GROUP_HEADS):
        cols = head_cols(head)
        number = own_ref[:, cols] + grow * acc[:, cols]
        mean = jnp.mean(number * number, axis=-1, keepdims=True)
        out_ref[:, cols] = (number * lax.rsqrt(mean + 1e-06) * gain_ref[0:1, cols]).astype(BF)
    other_ref[...] = product(out_ref, weight_ref, 2, 1).astype(BF)


def features_of(weight_ref, step, flip):
    place = lax.axis_index("head")
    chunk = (place // 2 + step) % SIDE * 2 + (place % 2 + flip) % 2
    return weight_ref[:, pl.ds(pl.multiple_of(chunk * CHUNK, HEAD_DIM), CHUNK)]


def product(normed_ref, weight_ref, step, flip):
    return jnp.dot(
        normed_ref[...], features_of(weight_ref, step, flip), preferred_element_type=F32
    )


def other_near_body(normed_ref, weight_ref, out_ref):
    @pl.loop(0, 3)
    def _(slot):
        step = jnp.where(slot == 0, 1, jnp.where(slot == 1, 3, 0))
        out_ref[slot] = product(normed_ref, weight_ref, step, 1).astype(BF)


def mine_far_body(normed_ref, weight_ref, other_ref, far_r, far_l):
    both = product(normed_ref, weight_ref, 2, 0) + other_ref[...].astype(F32)
    far_r[...] = both[:SPLIT].astype(BF)
    far_l[...] = both[SPLIT:].astype(BF)


def mine_near_body(normed_ref, weight_ref, other_ref, near_r, near_l, hold_r, hold_l, own_ref):
    both = product(normed_ref, weight_ref, 1, 0) + other_ref[0].astype(F32)
    hold_r[...] = both[:SPLIT]
    near_r[...] = both[SPLIT:].astype(BF)
    both = product(normed_ref, weight_ref, 3, 0) + other_ref[1].astype(F32)
    near_l[...] = both[:SPLIT].astype(BF)
    hold_l[...] = both[SPLIT:]
    own_ref[...] = product(normed_ref, weight_ref, 0, 0) + other_ref[2].astype(F32)


def pass_body(hold_r, far_r, hold_l, far_l, out_r, out_l):
    out_r[...] = (hold_r[...] + far_r[...].astype(F32)).astype(BF)
    out_l[...] = (hold_l[...] + far_l[...].astype(F32)).astype(BF)


def gather_body(own_ref, near_r, near_l, out_ref):
    near = jnp.concatenate([near_l[...], near_r[...]], axis=0).astype(F32)
    out_ref[...] = (own_ref[...] + near).T


def finish_body(own_ref, sum_r, sum_l, out_ref):
    sums = jnp.concatenate([sum_r[...], sum_l[...]], axis=0)
    out_ref[...] = (own_ref[...] + sums.T.astype(F32)).astype(BF)


def send(value, axis, pairs):
    return lax.ppermute(value, axis, pairs)


def per_device(queries, key_heads, value_heads, log_gates, norm_gain, out_weight):
    wide = GROUP_HEADS * HEAD_DIM
    after = lax.optimization_barrier
    payload, cum = kernel_call(
        prepare_body,
        (shape((PAY, 2 * HEAD_DIM), BF), shape((1, TOK), F32)),
        2**23,
        2**19,
        [pltpu.VMEM((TOK, HEAD_DIM), BF), pltpu.VMEM((1, TOK), F32), pltpu.SemaphoreType.DMA((3,))],
        vmem=60 * 2**20,
        in_specs=[pl.BlockSpec(memory_space=pltpu.HBM)] * 3,
    )(key_heads, value_heads, log_gates.reshape(1, TOK))
    row_back = send(payload, "ctx", CTX_Z[1])
    row_ahead = send(payload, "ctx", CTX_Z[-1])
    back0 = send(payload, "ctx", CTX_Y[1])
    ahead0 = send(payload, "ctx", CTX_Y[-1])
    block_flops = 4 * TOK * TOK * wide
    acc_shape, stat_shape = shape((TOK, wide), F32), shape((8, HEAD_DIM), F32)

    def scratch(blocks):
        return [pltpu.VMEM((blocks * TOK, HEAD_DIM), BF)] * 2

    row_far = send(row_back, "ctx", CTX_Z[1])
    middle = jnp.concatenate([row_back, row_ahead], axis=0)
    middle, own_keys = after((middle, key_heads))
    own = kernel_call(own_body, acc_shape, 8 * block_flops, 2**21, in_specs=[VMEM] * 4)(
        queries, own_keys, value_heads, cum
    )
    first0, own = after((back0, own))
    back12 = send(middle, "ctx", CTX_Y[1])
    ahead12 = send(middle, "ctx", CTX_Y[-1])
    first = kernel_call(
        first_body, shape((2, TOK, wide), F32), 2 * block_flops, 2**21, scratch(2), in_specs=[VMEM] * 3
    )(queries, first0, ahead0)
    pass0, row_far, first = after((ahead0, row_far, first))
    far0 = send(pass0, "ctx", CTX_Y[-1])
    acc, stat = kernel_call(
        row_body, (acc_shape, stat_shape), 24 * block_flops, 2**21, scratch(3), in_specs=[VMEM] * 5
    )(queries, payload, row_back, row_ahead, row_far)
    pass_back, pass_far, acc = after((back12, row_far, acc))
    far12 = send(pass_back, "ctx", CTX_Y[1])
    back3 = send(pass_back[PAY:], "ctx", CTX_Z[-1])
    far3 = send(pass_far, "ctx", CTX_Y[2])
    ahead3 = send(ahead12[:PAY], "ctx", CTX_Z[1])
    groups = kernel_call(
        middle_body,
        shape((2, 2, TOK, wide), F32),
        24 * block_flops,
        2**22,
        scratch(4),
        in_specs=[VMEM] * 6,
    )(queries, back0, back12, ahead0, ahead12, first)
    acc, stat = kernel_call(
        near_body,
        (shape((2, TOK, wide), F32), stat_shape),
        2 * block_flops,
        2**22,
        scratch(2),
        in_specs=[VMEM] * 10,
    )(queries, back0, back12, back3, ahead0, ahead12, ahead3, stat, acc, groups)
    chunk_flops = 2 * TOK * CHUNK * wide
    chunk = shape((TOK, CHUNK), BF)
    long_bf, long_f32 = shape((SPLIT, CHUNK), BF), shape((SPLIT, CHUNK), F32)
    short_bf, short_f32 = shape((TOK - SPLIT, CHUNK), BF), shape((TOK - SPLIT, CHUNK), F32)
    normed, other_far = kernel_call(
        last_body,
        (shape((TOK, wide), BF), chunk),
        4 * block_flops,
        2**22,
        [pltpu.VMEM((TOK, wide), F32), *scratch(4)],
        in_specs=[VMEM] * 10,
    )(queries, far0, far12, far3, stat, acc, own, cum, norm_gain.reshape(1, wide), out_weight)
    normed, other_far = after((normed, other_far))
    other_far = send(other_far, "head", CORE)
    other_near = kernel_call(
        other_near_body, shape((3, TOK, CHUNK), BF), 30 * chunk_flops, 2**21, in_specs=[VMEM] * 2
    )(normed, out_weight)
    other_near = send(other_near, "head", CORE)
    far_r, far_l = kernel_call(
        mine_far_body, (long_bf, short_bf), 30 * chunk_flops, 2**20, in_specs=[VMEM] * 3
    )(normed, out_weight, other_far)
    far_r = send(far_r, "head", HEAD_X[1])
    far_l = send(far_l, "head", HEAD_X[-1])
    near_r, near_l, hold_r, hold_l, own_sum = kernel_call(
        mine_near_body,
        (short_bf, long_bf, long_f32, short_f32, shape((TOK, CHUNK), F32)),
        3 * chunk_flops,
        2**22,
        in_specs=[VMEM] * 3,
    )(normed, out_weight, other_near)
    near_r = send(near_r, "head", HEAD_X[1])
    near_l = send(near_l, "head", HEAD_X[-1])
    sum_r, sum_l = kernel_call(pass_body, (long_bf, short_bf), 2**19, 2**21, in_specs=[VMEM] * 4)(
        hold_r, far_r, hold_l, far_l
    )
    sum_r = send(sum_r, "head", HEAD_X[1])
    sum_l = send(sum_l, "head", HEAD_X[-1])
    own_sum = kernel_call(
        gather_body, shape((CHUNK, TOK), F32), 2**20, 2**22, in_specs=[VMEM] * 3
    )(own_sum, near_r, near_l)
    return kernel_call(finish_body, shape((CHUNK, TOK), BF), 2**20, 2**22, in_specs=[VMEM] * 3)(
        own_sum, sum_r, sum_l
    )


def solution(mesh):
    return jax.shard_map(
        per_device,
        mesh=mesh,
        in_specs=(
            P("ctx", "head"),
            P("ctx", "head"),
            P("ctx", "head"),
            P("ctx", "head"),
            P("head"),
            P("head", None),
        ),
        out_specs=P("head", "ctx"),
        check_vma=False,
    )
```

```python
import jax
import jax.numpy as jnp
from jax import lax
from jax.experimental import pallas as pl
from jax.experimental.pallas import tpu as pltpu
from jax.sharding import PartitionSpec as P

HEAD_DIM = 128
GROUP_HEADS = 5
TOK = 512
PAY = TOK + 16
SIDE = 4
CHUNK = 640
SPLIT = TOK // 2
BF = jnp.bfloat16
F32 = jnp.float32
VMEM = pl.BlockSpec(memory_space=pltpu.VMEM)

CTX = SIDE * SIDE
CTX_Z = {d: [(i, (i // SIDE) * SIDE + (i + d) % SIDE) for i in range(CTX)] for d in (1, -1)}
CTX_Y = {d: [(i, (i + d * SIDE) % CTX) for i in range(CTX)] for d in (1, -1, 2)}
HEAD_X = {d: [(i, (i + 2 * d) % (2 * SIDE)) for i in range(2 * SIDE)] for d in (1, -1)}
CORE = [(i, i ^ 1) for i in range(2 * SIDE)]


def kernel_call(body, outs, flops, nbytes, scratch=(), vmem=24 * 2**20, **extra):
    return pl.pallas_call(
        body,
        out_shape=outs,
        in_specs=extra.pop("in_specs"),
        out_specs=extra.pop("out_specs", jax.tree.map(lambda _: VMEM, outs)),
        scratch_shapes=list(scratch),
        compiler_params=pltpu.CompilerParams(vmem_limit_bytes=vmem),
        cost_estimate=pl.CostEstimate(flops=flops, bytes_accessed=nbytes, transcendentals=0),
        **extra,
    )


def shape(dims, kind):
    return jax.ShapeDtypeStruct(dims, kind)


def column(row):
    return jnp.broadcast_to(row, (HEAD_DIM, TOK)).T[:, :1]


def prepare_body(key_hbm, value_hbm, gate_hbm, out_ref, cum_ref, value_ref, gate_ref, sems):
    copies = [
        pltpu.make_async_copy(gate_hbm, gate_ref, sems.at[0]),
        pltpu.make_async_copy(value_hbm, value_ref, sems.at[1]),
        pltpu.make_async_copy(key_hbm, out_ref.at[pl.ds(0, TOK), pl.ds(0, HEAD_DIM)], sems.at[2]),
    ]
    for copy in copies:
        copy.start()
    copies[0].wait()
    gates = gate_ref[...]
    top = gates.astype(BF).astype(F32)
    mid = (gates - top).astype(BF).astype(F32)
    rows = lax.broadcasted_iota(jnp.int32, (16, TOK), 0)
    parts = jnp.where(rows == 0, top, jnp.where(rows == 1, mid, gates - top - mid))
    parts = jnp.where(rows < 3, parts, 0.0).astype(BF)
    source = lax.broadcasted_iota(jnp.int32, (TOK, TOK), 0)
    place = lax.broadcasted_iota(jnp.int32, (TOK, TOK), 1)
    upto = jnp.where(source <= place, 1.0, 0.0).astype(BF)
    sums = jnp.dot(parts, upto, preferred_element_type=F32)
    cum = jnp.sum(sums, axis=0, keepdims=True)
    cum_ref[...] = cum
    total = cum[:, TOK - 1 :]
    copies[1].wait()
    out_ref[:TOK, HEAD_DIM:] = (value_ref[...].astype(F32) * jnp.exp(total - column(cum))).astype(BF)
    top = total.astype(BF).astype(F32)
    mid = (total - top).astype(BF).astype(F32)
    rows = lax.broadcasted_iota(jnp.int32, (16, HEAD_DIM), 0)
    lanes = lax.broadcasted_iota(jnp.int32, (16, HEAD_DIM), 1)
    tile = jnp.where(lanes == 0, top, jnp.where(lanes == 1, mid, jnp.where(lanes == 2, total - top - mid, 0.0)))
    out_ref[TOK:, :HEAD_DIM] = jnp.where(rows == 0, tile, 0.0).astype(BF)
    out_ref[TOK:, HEAD_DIM:] = jnp.zeros((16, HEAD_DIM), BF)
    copies[2].wait()


def inner(query, key):
    return lax.dot_general(query, key, (((1,), (1,)), ((), ())), preferred_element_type=F32)


def head_cols(head):
    return slice(head * HEAD_DIM, (head + 1) * HEAD_DIM)


def own_body(query_ref, key_ref, value_ref, cum_ref, out_ref):
    cum_col = column(cum_ref[...])
    half = TOK // 2
    for part in range(2):
        rows = slice(part * half, (part + 1) * half)
        seen = (part + 1) * half
        place = part * half + lax.broadcasted_iota(jnp.int32, (half, seen), 0)
        source = lax.broadcasted_iota(jnp.int32, (half, seen), 1)
        decay = jnp.exp(jnp.minimum(cum_col[rows] - cum_ref[0:1, :seen], 0.0))
        decay = jnp.where(place >= source, decay, 0.0)
        for head in range(GROUP_HEADS):
            scores = inner(query_ref[rows, head_cols(head)], key_ref[:seen, :])
            scores = (scores * scores * decay).astype(BF)
            out_ref[rows, head_cols(head)] = jnp.dot(
                scores, value_ref[:seen, :], preferred_element_type=F32
            )


def total_of(ref, slot):
    tile = ref[slot * PAY + TOK : (slot + 1) * PAY, :HEAD_DIM].astype(F32)
    return jnp.sum(jnp.sum(tile, axis=1, keepdims=True), axis=0, keepdims=True)


def slot_places(place_z):
    return [place_z, (place_z + 3) % SIDE, (place_z + 1) % SIDE, (place_z + 2) % SIDE]


def gated(condition, value):
    return jnp.where(condition, value, jnp.zeros_like(value))


def later_sums(places, totals):
    return [
        sum(gated(places[i] > places[k], totals[i]) for i in range(SIDE) if i != k)
        for k in range(SIDE)
    ]


def stage(slot, log_decay, place, keys, values):
    ref, index = slot
    rows = slice(index * PAY, index * PAY + TOK)
    target = slice(place * TOK, (place + 1) * TOK)
    keys[target, :] = ref[rows, :HEAD_DIM]
    values[target, :] = (ref[rows, HEAD_DIM:].astype(F32) * jnp.exp(log_decay)).astype(BF)


def attend(query_ref, keys, values, start, size, acc_ref):
    rows = pl.ds(pl.multiple_of(start, size), size)
    key, value = keys[rows, :], values[rows, :]
    for head in range(GROUP_HEADS):
        scores = inner(query_ref[:, head_cols(head)], key)
        scores = (scores * scores).astype(BF)
        acc_ref[:, head_cols(head)] += jnp.dot(scores, value, preferred_element_type=F32)


def row_body(query_ref, own_ref, back_ref, ahead_ref, far_ref, acc_ref, stat_ref, keys, values):
    place_z = lax.axis_index("ctx") % SIDE
    places = slot_places(place_z)
    refs = [own_ref, back_ref, ahead_ref, far_ref]
    totals = [total_of(ref, 0) for ref in refs]
    acc_ref[...] = jnp.zeros_like(acc_ref)
    before = sum(gated(places[k] < place_z, totals[k]) for k in range(1, SIDE))
    stat_ref[...] = jnp.broadcast_to(before, stat_ref.shape)
    for k in range(1, SIDE):
        log_decay = sum(
            gated((places[i] > places[k]) & (places[i] < place_z), totals[i])
            for i in range(1, SIDE)
            if i != k
        )
        stage((refs[k], 0), log_decay, k - 1, keys, values)

    @pl.loop(0, SIDE - 1)
    def _(i):
        turn = jnp.where(i == 0, 3, i)
        is_before = (place_z + turn) % SIDE < place_z

        @pl.when(is_before)
        def _():
            attend(query_ref, keys, values, i * TOK, TOK, acc_ref)


def wanted(row):
    place_y = lax.axis_index("ctx") // SIDE
    return jnp.where(row == 0, place_y >= 1, place_y == SIDE - 1)


def first_body(query_ref, back_ref, ahead_ref, acc_ref, keys, values):
    zero = jnp.zeros((1, 1), F32)
    stage((back_ref, 0), zero, 0, keys, values)
    stage((ahead_ref, 0), zero, 1, keys, values)
    acc_ref[...] = jnp.zeros_like(acc_ref)

    @pl.loop(0, 2)
    def _(row):
        @pl.when(wanted(row))
        def _():
            attend(query_ref, keys, values, row * TOK, TOK, acc_ref.at[row])


def middle_body(query_ref, back0, back12, ahead0, ahead12, first_ref, acc_ref, keys, values):
    places = slot_places(lax.axis_index("ctx") % SIDE)
    later = [places[SIDE - 1] > places[k] for k in range(SIDE - 1)]
    for row, slots in enumerate(([(back0, 0), (back12, 0), (back12, 1)], [(ahead0, 0), (ahead12, 0), (ahead12, 1)])):
        totals = [total_of(*slot) for slot in slots]
        decays = [
            sum(gated(places[i] > places[k], totals[i]) for i in range(SIDE - 1) if i != k)
            for k in range(SIDE - 1)
        ]
        for k in (1, 2):
            stage(slots[k], decays[k], 2 * row + k - 1, keys, values)
        first = jnp.exp(decays[0]) * first_ref[row]
        acc_ref[row, 0] = gated(~later[0], first)
        acc_ref[row, 1] = gated(later[0], first)

    @pl.loop(0, 4)
    def _(i):
        row, slot = i // 2, 1 + i % 2
        group = jnp.where(slot == 1, later[1], later[2]).astype(jnp.int32)

        @pl.when(wanted(row))
        def _():
            attend(query_ref, keys, values, i * TOK, TOK, acc_ref.at[row, group])


def row_slots(first, middle, far):
    return [(first, 0), (middle, 0), (middle, 1), (far, 0)]


def near_body(
    query_ref, back0, back12, back3, ahead0, ahead12, ahead3, stat_ref, acc_in, groups,
    acc_ref, out_stat, keys, values
):
    places = slot_places(lax.axis_index("ctx") % SIDE)
    before = stat_ref[0:1, 0:1]
    for row, slots in enumerate((row_slots(back0, back12, back3), row_slots(ahead0, ahead12, ahead3))):
        totals = [total_of(*slot) for slot in slots]
        last = sum(gated(places[i] > places[SIDE - 1], totals[i]) for i in range(SIDE - 1))
        base = before if row == 0 else jnp.zeros_like(before)
        stage(slots[SIDE - 1], base + last, row, keys, values)
        both = jnp.exp(base) * groups[row, 0] + jnp.exp(base + totals[SIDE - 1]) * groups[row, 1]
        acc_ref[row] = acc_in[...] + both if row == 0 else both
        if row == 0:
            out_stat[...] = jnp.broadcast_to(before + sum(totals), out_stat.shape)

    @pl.loop(0, 2)
    def _(row):
        @pl.when(wanted(row))
        def _():
            attend(query_ref, keys, values, row * TOK, TOK, acc_ref.at[row])


def last_body(
    query_ref, far0, far12, far3, stat_ref, acc_in, own_ref, cum_ref, gain_ref, weight_ref,
    out_ref, other_ref, acc, keys, values
):
    index = lax.axis_index("ctx")
    place_y, places = index // SIDE, slot_places(index % SIDE)
    before = stat_ref[0:1, 0:1]
    slots = row_slots(far0, far12, far3)
    totals = [total_of(*slot) for slot in slots]
    later = later_sums(places, totals)
    for k in range(SIDE):
        stage(slots[k], before + later[k], k, keys, values)
    acc[...] = acc_in[0]

    @pl.when(place_y == SIDE - 1)
    def _():
        acc[...] += jnp.exp(before + sum(totals)) * acc_in[1]

    @pl.when(place_y >= 2)
    def _():
        attend(query_ref, keys, values, 0, SIDE * TOK, acc)

    grow = jnp.exp(column(cum_ref[...]))
    for head in range(GROUP_HEADS):
        cols = head_cols(head)
        number = own_ref[:, cols] + grow * acc[:, cols]
        mean = jnp.mean(number * number, axis=-1, keepdims=True)
        out_ref[:, cols] = (number * lax.rsqrt(mean + 1e-06) * gain_ref[0:1, cols]).astype(BF)
    other_ref[...] = product(out_ref, weight_ref, 2, 1).astype(BF)


def features_of(weight_ref, step, flip):
    place = lax.axis_index("head")
    chunk = (place // 2 + step) % SIDE * 2 + (place % 2 + flip) % 2
    return weight_ref[:, pl.ds(pl.multiple_of(chunk * CHUNK, HEAD_DIM), CHUNK)]


def product(normed_ref, weight_ref, step, flip):
    return jnp.dot(
        normed_ref[...], features_of(weight_ref, step, flip), preferred_element_type=F32
    )


def other_near_body(normed_ref, weight_ref, out_ref):
    @pl.loop(0, 2)
    def _(slot):
        out_ref[slot] = product(normed_ref, weight_ref, jnp.where(slot == 0, 1, 3), 1).astype(BF)


def mine_far_body(normed_ref, weight_ref, other_ref, far_r, far_l):
    both = product(normed_ref, weight_ref, 2, 0) + other_ref[...].astype(F32)
    far_r[...] = both[:SPLIT].astype(BF)
    far_l[...] = both[SPLIT:].astype(BF)


def mine_near_body(normed_ref, weight_ref, other_ref, near_r, near_l, hold_r, hold_l, own_other, own_ref):
    both = product(normed_ref, weight_ref, 1, 0) + other_ref[0].astype(F32)
    hold_r[...] = both[:SPLIT]
    near_r[...] = both[SPLIT:].astype(BF)
    both = product(normed_ref, weight_ref, 3, 0) + other_ref[1].astype(F32)
    near_l[...] = both[:SPLIT].astype(BF)
    hold_l[...] = both[SPLIT:]
    own_other[...] = product(normed_ref, weight_ref, 0, 1).astype(BF)
    own_ref[...] = product(normed_ref, weight_ref, 0, 0)


def pass_body(hold_r, far_r, hold_l, far_l, out_r, out_l):
    out_r[...] = (hold_r[...] + far_r[...].astype(F32)).astype(BF)
    out_l[...] = (hold_l[...] + far_l[...].astype(F32)).astype(BF)


def gather_body(own_ref, other_ref, near_r, near_l, out_ref):
    near = jnp.concatenate([near_l[...], near_r[...]], axis=0).astype(F32)
    out_ref[...] = (own_ref[...] + other_ref[...].astype(F32) + near).T


def finish_body(own_ref, sum_r, sum_l, out_ref):
    sums = jnp.concatenate([sum_r[...], sum_l[...]], axis=0)
    out_ref[...] = (own_ref[...] + sums.T.astype(F32)).astype(BF)


def send(value, axis, pairs):
    return lax.ppermute(value, axis, pairs)


def per_device(queries, key_heads, value_heads, log_gates, norm_gain, out_weight):
    wide = GROUP_HEADS * HEAD_DIM
    after = lax.optimization_barrier
    payload, cum = kernel_call(
        prepare_body,
        (shape((PAY, 2 * HEAD_DIM), BF), shape((1, TOK), F32)),
        2**23,
        2**19,
        [pltpu.VMEM((TOK, HEAD_DIM), BF), pltpu.VMEM((1, TOK), F32), pltpu.SemaphoreType.DMA((3,))],
        vmem=60 * 2**20,
        in_specs=[pl.BlockSpec(memory_space=pltpu.HBM)] * 3,
    )(key_heads, value_heads, log_gates.reshape(1, TOK))
    row_back = send(payload, "ctx", CTX_Z[1])
    row_ahead = send(payload, "ctx", CTX_Z[-1])
    back0 = send(payload, "ctx", CTX_Y[1])
    ahead0 = send(payload, "ctx", CTX_Y[-1])
    block_flops = 4 * TOK * TOK * wide
    acc_shape, stat_shape = shape((TOK, wide), F32), shape((8, HEAD_DIM), F32)

    def scratch(blocks):
        return [pltpu.VMEM((blocks * TOK, HEAD_DIM), BF)] * 2

    row_far = send(row_back, "ctx", CTX_Z[1])
    middle = jnp.concatenate([row_back, row_ahead], axis=0)
    middle, own_keys = after((middle, key_heads))
    own = kernel_call(own_body, acc_shape, 8 * block_flops, 2**21, in_specs=[VMEM] * 4)(
        queries, own_keys, value_heads, cum
    )
    first0, own = after((back0, own))
    back12 = send(middle, "ctx", CTX_Y[1])
    ahead12 = send(middle, "ctx", CTX_Y[-1])
    first = kernel_call(
        first_body, shape((2, TOK, wide), F32), 2 * block_flops, 2**21, scratch(2), in_specs=[VMEM] * 3
    )(queries, first0, ahead0)
    pass0, row_far, first = after((ahead0, row_far, first))
    far0 = send(pass0, "ctx", CTX_Y[-1])
    acc, stat = kernel_call(
        row_body, (acc_shape, stat_shape), 24 * block_flops, 2**21, scratch(3), in_specs=[VMEM] * 5
    )(queries, payload, row_back, row_ahead, row_far)
    pass_back, pass_far, acc = after((back12, row_far, acc))
    far12 = send(pass_back, "ctx", CTX_Y[1])
    back3 = send(pass_back[PAY:], "ctx", CTX_Z[-1])
    far3 = send(pass_far, "ctx", CTX_Y[2])
    ahead3 = send(ahead12[:PAY], "ctx", CTX_Z[1])
    groups = kernel_call(
        middle_body,
        shape((2, 2, TOK, wide), F32),
        24 * block_flops,
        2**22,
        scratch(4),
        in_specs=[VMEM] * 6,
    )(queries, back0, back12, ahead0, ahead12, first)
    acc, stat = kernel_call(
        near_body,
        (shape((2, TOK, wide), F32), stat_shape),
        2 * block_flops,
        2**22,
        scratch(2),
        in_specs=[VMEM] * 10,
    )(queries, back0, back12, back3, ahead0, ahead12, ahead3, stat, acc, groups)
    chunk_flops = 2 * TOK * CHUNK * wide
    chunk = shape((TOK, CHUNK), BF)
    long_bf, long_f32 = shape((SPLIT, CHUNK), BF), shape((SPLIT, CHUNK), F32)
    short_bf, short_f32 = shape((TOK - SPLIT, CHUNK), BF), shape((TOK - SPLIT, CHUNK), F32)
    normed, other_far = kernel_call(
        last_body,
        (shape((TOK, wide), BF), chunk),
        4 * block_flops,
        2**22,
        [pltpu.VMEM((TOK, wide), F32), *scratch(4)],
        in_specs=[VMEM] * 10,
    )(queries, far0, far12, far3, stat, acc, own, cum, norm_gain.reshape(1, wide), out_weight)
    normed, other_far = after((normed, other_far))
    other_far = send(other_far, "head", CORE)
    other_near = kernel_call(
        other_near_body, shape((2, TOK, CHUNK), BF), 30 * chunk_flops, 2**21, in_specs=[VMEM] * 2
    )(normed, out_weight)
    other_near = send(other_near, "head", CORE)
    far_r, far_l = kernel_call(
        mine_far_body, (long_bf, short_bf), 30 * chunk_flops, 2**20, in_specs=[VMEM] * 3
    )(normed, out_weight, other_far)
    normed, far_r, far_l = after((normed, far_r, far_l))
    far_r = send(far_r, "head", HEAD_X[1])
    far_l = send(far_l, "head", HEAD_X[-1])
    near_r, near_l, hold_r, hold_l, other_own, own_sum = kernel_call(
        mine_near_body,
        (short_bf, long_bf, long_f32, short_f32, chunk, shape((TOK, CHUNK), F32)),
        4 * chunk_flops,
        2**22,
        in_specs=[VMEM] * 3,
    )(normed, out_weight, other_near)
    near_r = send(near_r, "head", HEAD_X[1])
    near_l = send(near_l, "head", HEAD_X[-1])
    other_own = send(other_own, "head", CORE)
    sum_r, sum_l = kernel_call(pass_body, (long_bf, short_bf), 2**19, 2**21, in_specs=[VMEM] * 4)(
        hold_r, far_r, hold_l, far_l
    )
    sum_r = send(sum_r, "head", HEAD_X[1])
    sum_l = send(sum_l, "head", HEAD_X[-1])
    own_sum = kernel_call(
        gather_body, shape((CHUNK, TOK), F32), 2**20, 2**22, in_specs=[VMEM] * 4
    )(own_sum, other_own, near_r, near_l)
    return kernel_call(finish_body, shape((CHUNK, TOK), BF), 2**20, 2**22, in_specs=[VMEM] * 3)(
        own_sum, sum_r, sum_l
    )


def solution(mesh):
    return jax.shard_map(
        per_device,
        mesh=mesh,
        in_specs=(
            P("ctx", "head"),
            P("ctx", "head"),
            P("ctx", "head"),
            P("ctx", "head"),
            P("head"),
            P("head", None),
        ),
        out_specs=P("head", "ctx"),
        check_vma=False,
    )
```
